512 devices in a mesh: dp: 16 (over z), seq: 32 (over x, y, core).
Axes of the slice: x: 4, y: 4, z: 16, core: 2. Of those that a mesh axis runs over, the one named last changes fastest.
Arguments:
- hidden_states: bfloat16 [1024, 128, 1152], P(('dp', 'seq')), may hold values from -6 to 6
- spatial_qkv: bfloat16 [1024, 128, 3456], P(('dp', 'seq')), may hold values from -6 to 6
- spatial_out_weight: bfloat16 [1152, 1152], P('dp'), may hold values from -0.1875 to 0.1875
- temporal_qkv_weight: bfloat16 [1152, 3456], P('dp'), may hold values from -1 to 1, as said below
- modulation: float32 [4, 1152], replicated, may hold values from -4 to 4
- video_ids: int32 [1024], P(('dp', 'seq')), may hold values from 0 to 63, never falling along the last dimension, each value on 1 to 64 neighbouring positions
Outputs:
- block_output: bfloat16 [1024, 128, 1152], P(('dp', 'seq'))
The draws below stay inside these ranges and needn't reach their ends.
Inputs may be any that keep to these rules, and one draw needn't show every extreme that they name: `video_ids`: frames of one video are consecutive; a video has 1 to 64 frames, and some video has exactly 64. `temporal_qkv_weight`: a matrix scaled by the square root of its fan-in 1152.
All inputs are finite; a program needn't handle non-finite values.
Results may differ from the reference program's by a relative error of at most 0.04.
Values may be sent and summed in bfloat16 or wider, within the bound.
A program may use at most 64 MiB of HBM per device.

```python
import math
import jax
import jax.numpy as jnp
import numpy as np
from jax import lax

HEADS = 16
HD = 72
D = 1152
P_SIZE = 128
GF = 64
FRAMES = 1024
VIDEOS = 64
N_DP = 16


def draw_spatial_qkv(key, part):
    key = jax.random.fold_in(key, 11)
    return jax.random.truncated_normal(key, -6.0, 6.0, (FRAMES, P_SIZE, 3 * D), jnp.float32).astype(jnp.bfloat16)


def draw_temporal_qkv_weight(key, part):
    key = jax.random.fold_in(key, 12)
    return (jax.random.truncated_normal(key, -6.0, 6.0, (D, 3 * D), jnp.float32) / math.sqrt(D)).astype(jnp.bfloat16)


def draw_modulation(key, part):
    key = jax.random.fold_in(key, 13)
    return jax.random.truncated_normal(key, -4.0, 4.0, (4, D), jnp.float32)


def level_of(key, extent, cuts, low, high):
    loudness, own = 1.0, jax.random.fold_in(key, 6)
    for axis_at, blocks in cuts:
        heights = jnp.exp(jax.random.uniform(jax.random.fold_in(own, axis_at), (blocks,), jnp.float32, low / len(cuts), high / len(cuts)))
        loudness = loudness * jnp.repeat(heights, extent[axis_at] // blocks).reshape([-1 if axis == axis_at else 1 for axis in range(len(extent))])
    return loudness


def split_up(count, total, limit, slope):
    loads = [(1 << 20) // math.isqrt(standing ** slope) + 1 for standing in range(2, count + 1)]
    surplus, holding = total - limit - (count - 1), [1] * (count - 1)
    while surplus > 0:
        candidates = [i for i in range(count - 1) if holding[i] < limit]
        pool, remaining = sum([loads[i] for i in candidates]), surplus
        for i in candidates:
            addition = min(limit - holding[i], max(1, remaining * loads[i] // pool), surplus)
            holding[i] = holding[i] + addition
            surplus = surplus - addition
    return np.array([limit] + holding)


def uneven_parts(own_key, number_of, total, most, lean):
    if number_of == 2:
        one = jax.random.randint(own_key, (), max(1, total - most), min(most, total - 1) + 1)
        return jnp.stack([one, total - one])
    sizes = jnp.asarray(split_up(number_of, total, most, lean), jnp.int32)
    twos = (number_of - 1) // 2
    giver, sink = sizes[1:1 + 2 * twos:2], sizes[2:2 + 2 * twos:2]
    margin = jnp.minimum(giver - 1, most - sink)
    moved = jax.random.randint(jax.random.fold_in(own_key, 1), (twos,), 0, 1 << 20) % (margin + 1)
    sizes = sizes.at[1:1 + 2 * twos:2].set(giver - moved).at[2:2 + 2 * twos:2].set(sink + moved)
    return sizes[jax.random.permutation(jax.random.fold_in(own_key, 2), number_of)]


def gaussian(own_key, dims, deviation, most, cuts=(), kind=jnp.bfloat16):
    factor_of = level_of(own_key, dims, cuts, -0.22, 0.18) if cuts else 1.0
    values = jax.random.normal(own_key, dims, jnp.float32) * deviation * factor_of
    return jnp.minimum(jnp.maximum(values, -most), most).astype(kind)


def setup_inputs(seed: int = 0) -> dict:
    key_list = jax.random.split(jax.random.key(seed), 7)
    hidden_states = gaussian(key_list[0], (FRAMES, P_SIZE, D), 1.0, 6.0, ((0, 512),))
    spatial_qkv = draw_spatial_qkv(jax.random.fold_in(key_list[6], 71), 0)
    spatial_out_weight = gaussian(key_list[2], (D, D), D ** -0.5, 0.1875, ((0, 16),))
    temporal_qkv_weight = draw_temporal_qkv_weight(jax.random.fold_in(key_list[6], 71), 0)
    modulation = draw_modulation(jax.random.fold_in(key_list[6], 71), 0)
    video_ids = jnp.searchsorted(jnp.cumsum(uneven_parts(key_list[5], VIDEOS, FRAMES, GF, 2)), jnp.arange(FRAMES), side="right").astype(jnp.int32)
    return dict(hidden_states=hidden_states, spatial_qkv=spatial_qkv, spatial_out_weight=spatial_out_weight, temporal_qkv_weight=temporal_qkv_weight, modulation=modulation, video_ids=video_ids)


NEG = -1e+30
EPS = 1e-06

def softmax_weights(scores):
    top = lax.optimization_barrier(jnp.max(scores, axis=-1, keepdims=True))
    powers = jnp.exp(scores - top)
    return (powers / lax.optimization_barrier(jnp.sum(powers, axis=-1, keepdims=True))).astype(jnp.bfloat16)

def reference(hidden_states, spatial_qkv, spatial_out_weight, temporal_qkv_weight, modulation, video_ids):
    scale = 1.0 / math.sqrt(HD)

    def spatial_frame(block):
        parts = block.astype(jnp.float32).reshape(P_SIZE, 3, HEADS, HD)
        scores = jnp.einsum('qhd,khd->hqk', parts[:, 0], parts[:, 1]) * scale
        weights = lax.optimization_barrier(softmax_weights(scores)).astype(jnp.float32)
        result = jnp.einsum('hqk,khd->qhd', weights, parts[:, 2])
        return result.reshape(P_SIZE, D).astype(jnp.bfloat16)
    spatial = lax.map(spatial_frame, spatial_qkv).reshape(FRAMES * P_SIZE, D)
    projected = jnp.dot(spatial, spatial_out_weight, preferred_element_type=jnp.float32)
    residual = (hidden_states.reshape(FRAMES * P_SIZE, D).astype(jnp.float32) + modulation[0] * projected).astype(jnp.bfloat16)
    values32 = residual.astype(jnp.float32)
    centred = values32 - lax.optimization_barrier(jnp.mean(values32, axis=-1, keepdims=True))
    variance = lax.optimization_barrier(jnp.mean(centred * centred, axis=-1, keepdims=True))
    normed = (centred * lax.rsqrt(variance + EPS) * (1.0 + modulation[2]) + modulation[1]).astype(jnp.bfloat16)
    temporal_qkv = jnp.dot(normed, temporal_qkv_weight, preferred_element_type=jnp.float32).astype(jnp.bfloat16)
    temporal_qkv = temporal_qkv.reshape(N_DP, GF, P_SIZE, 3 * D)
    empty_group = jnp.zeros((1, GF, P_SIZE, 2 * D), jnp.bfloat16)
    keyvals = jnp.concatenate([empty_group, temporal_qkv[..., D:], empty_group], axis=0)
    outside = jnp.full((1, GF), -1, jnp.int32)
    padded_ids = jnp.concatenate([outside, video_ids.reshape(N_DP, GF).astype(jnp.int32), outside], axis=0)

    def temporal_group(group):
        queries = lax.dynamic_index_in_dim(temporal_qkv, group, 0, keepdims=False)[..., :D]
        queries = queries.astype(jnp.float32).reshape(GF, P_SIZE, HEADS, HD)
        block = lax.dynamic_slice_in_dim(keyvals, group, 3, 0).reshape(3 * GF, P_SIZE, 2 * D).astype(jnp.float32)
        keys = block[..., :D].reshape(3 * GF, P_SIZE, HEADS, HD)
        values = block[..., D:].reshape(3 * GF, P_SIZE, HEADS, HD)
        key_ids = lax.dynamic_slice_in_dim(padded_ids, group, 3, 0).reshape(3 * GF)
        query_ids = lax.dynamic_index_in_dim(padded_ids, group + 1, 0, keepdims=False)
        scores = jnp.einsum('iphd,jphd->phij', queries, keys) * scale
        same = query_ids[:, None] == key_ids[None, :]
        scores = jnp.where(same[None, None], scores, NEG)
        weights = lax.optimization_barrier(softmax_weights(scores)).astype(jnp.float32)
        result = jnp.einsum('phij,jphd->iphd', weights, values)
        return result.reshape(GF, P_SIZE, D).astype(jnp.bfloat16)
    temporal = lax.map(temporal_group, jnp.arange(N_DP, dtype=jnp.int32)).reshape(FRAMES * P_SIZE, D)
    output = residual.astype(jnp.float32) + modulation[3] * temporal.astype(jnp.float32)
    return output.astype(jnp.bfloat16).reshape(FRAMES, P_SIZE, D)
```

```python
import math

import jax
import jax.numpy as jnp
from jax import lax
from jax.experimental import pallas as pl
from jax.experimental.pallas import tpu as pltpu
from jax.sharding import PartitionSpec as P

HEADS = 16
HD = 72
D = 1152
NEG = -1e30
EPS = 1e-06
SCALE = 1.0 / math.sqrt(HD)

NZ = 16
ROWS = 72
CHIPS = 16
POS = 8
BLK = 16
TOK = 1280
HALF = 640
MESH = pl.DeviceIdType.MESH
BF = jnp.bfloat16
F32 = jnp.float32


def iota(shape, dim):
    return lax.broadcasted_iota(jnp.int32, shape, dim)


def dot(a, b):
    return jnp.dot(a, b, preferred_element_type=F32)


def dot_t(a, b):
    return lax.dot_general(a, b, (((1,), (1,)), ((), ())), preferred_element_type=F32)


def softmax(scores):
    top = jnp.max(scores, axis=-1, keepdims=True)
    powers = jnp.exp(scores - top)
    return (powers * (1.0 / jnp.sum(powers, axis=-1, keepdims=True))).astype(BF)


def pair_masks(pair, rows):
    lane = iota((rows, 256), 1)
    low = 16 * pair
    first = (lane >= low) & (lane < low + HD)
    second = (lane >= low + HD) & (lane < low + 2 * HD)
    return first, second


def frame_order(rows):
    core, chip, two, pos = rows // 256, (rows % 256) // 16, (rows % 16) // 8, rows % 8
    return pos * 64 + chip * 4 + core * 2 + two


def kernel(
    hid_ref, qkv_ref, wo_ref, wt_ref, mod_ref, ids_ref, out_ref,
    w8, wxo, wxq, wout, wqkv, sp, res, ns, xb, xp, qs, kv, tt, tb, rb, perm, perm_t,
    zs, zr, xso, xro, xsq, xrq, ls, lr, a_s, a_r, hs, hr, ss, sr, r_s, r_r,
):
    z, seq = lax.axis_index("dp"), lax.axis_index("seq")
    core, chip = seq % 2, seq // 2
    x, y = chip // 4, chip % 4
    up, down, sib = (z + 1) % NZ, (z + NZ - 1) % NZ, chip * 2 + (1 - core)

    def copy(src, dst, send, recv, dev):
        return pltpu.make_async_remote_copy(
            src_ref=src, dst_ref=dst, send_sem=send, recv_sem=recv, device_id=dev, device_id_type=MESH
        )

    barrier = pltpu.get_barrier_semaphore()

    def greet(j, _):
        pl.semaphore_signal(barrier, inc=1, device_id=(z, (seq + j) % 32), device_id_type=MESH)
        return 0

    lax.fori_loop(1, 32, greet, 0)
    pl.semaphore_signal(barrier, inc=1, device_id=(up, seq), device_id_type=MESH)
    pl.semaphore_signal(barrier, inc=1, device_id=(down, seq), device_id_type=MESH)

    for q in range(4):
        wxo[core, q, z] = wo_ref[:, pl.ds(pl.multiple_of(256 * q + 128 * core, 128), 128)]
        for u in range(4):
            n = min(4 * q + u, 14)
            lanes = pl.ds(pl.multiple_of((n // 5) * D + 128 * (n % 5) + 512 * core, 128), 128)
            wxq[q, z, :, 128 * u : 128 * u + 128] = wt_ref[:, lanes]
    w8[z] = wo_ref[:, 1024:1152]
    sp[...] = jnp.zeros_like(sp)
    pl.semaphore_wait(barrier, 33)

    def quarter(k):
        odd = k % 2
        return y * (1 - odd) + x * odd

    def ring(kind, way, step, k):
        dev = (up, seq) if way == 0 else (down, seq)
        ref = (wxo.at[core, quarter(k), k], w8.at[k], wxq.at[quarter(k), k])[kind]
        return copy(ref, ref, zs.at[way, kind, step], zr.at[way, kind, step], dev)

    def sent(way, step):
        return (z + NZ - step) % NZ if way == 0 else (z + step) % NZ

    def across(kind, k, j):
        odd = k % 2
        dev = (z, (((x + j * odd) % 4) * 4 + (y + j * (1 - odd)) % 4) * 2 + core)
        q = quarter(k)
        if kind == 0:
            ref, send, recv = wxo.at[core, q, k], xso.at[k, j - 1], xro.at[q, k]
        else:
            ref, send, recv = wxq.at[q, k], xsq.at[k, j - 1], xrq.at[q, k]
        return copy(ref, ref, send, recv, dev)

    def arrived(kind, k, j):
        q = (quarter(k) + j) % 4
        if kind == 0:
            ref, send, recv = wxo.at[core, q, k], xso.at[k, j - 1], xro.at[q, k]
        else:
            ref, send, recv = wxq.at[q, k], xsq.at[k, j - 1], xrq.at[q, k]
        copy(ref, ref, send, recv, (z, sib)).wait_recv()

    def spatial_pair(f, pair):
        off = pl.multiple_of(128 * pair, 128)
        first, second = pair_masks(pair, 128)
        q = qkv_ref[f, :, pl.ds(off, 256)]
        k = qkv_ref[f, :, pl.ds(pl.multiple_of(D + off, 128), 256)]
        v = qkv_ref[f, :, pl.ds(pl.multiple_of(2 * D + off, 128), 256)]
        both = jnp.concatenate([q * first.astype(F32).astype(BF), q * second.astype(F32).astype(BF)], axis=0)
        o = dot(softmax(dot_t(both, k) * SCALE), v)
        rows = slice(128 * f, 128 * f + 128)
        old = sp[rows, pl.ds(off, 256)].astype(F32)
        sp[rows, pl.ds(off, 256)] = jnp.where(first, o[:128], jnp.where(second, o[128:], old)).astype(BF)

    for way in range(2):
        for kind in range(3):
            ring(kind, way, 0, z).start()

    def ring_step(step, _):
        for kinds, f in (((0, 1), 0), ((2,), 1)):
            spatial_pair(f, step)
            for way, steps in ((0, 8), (1, 7)):

                @pl.when(step < steps)
                def _():
                    k = sent(way, step + 1)
                    for kind in kinds:
                        ring(kind, way, step, k).wait_recv()

                    @pl.when(step < steps - 1)
                    def _():
                        for kind in kinds:
                            ring(kind, way, step + 1, k).start()

                    if kinds[0] == 0:
                        for j in range(1, 4):
                            across(0, k, j).start()
                    elif way == 0:
                        for j in range(1, 4):
                            across(2, k, j).start()

        return 0

    lax.fori_loop(0, 8, ring_step, 0)

    def wait_out(i, _):
        for j in range(1, 4):
            arrived(0, (z + i) % NZ, j)
        return 0

    lax.fori_loop(1, NZ, wait_out, 0)
    to_sib = copy(wxo.at[core], wxo.at[core], ls, lr, (z, sib))
    to_sib.start()
    copy(wxo.at[1 - core], wxo.at[1 - core], ls, lr, (z, sib)).wait_recv()

    for t in range(9):
        piece = w8[...] if t == 8 else wxo[t % 2, t // 2]
        wout[:, 128 * t : 128 * t + 128] = piece.astype(F32).reshape(D, 128).astype(BF)
    for low, wide in ((0, 256), (256, 256), (512, 256), (768, 256), (1024, 128)):
        lanes = slice(low, low + wide)
        projected = dot(sp[...], wout[:, lanes])
        res[:, lanes] = (
            hid_ref[:, :, lanes].reshape(256, wide).astype(F32) + mod_ref[0:1, lanes] * projected
        ).astype(BF)

    first_id, second_id = ids_ref[0].astype(F32), ids_ref[1].astype(F32)
    number = jnp.where(iota((BLK, 128), 0) < POS, first_id, second_id).astype(BF)

    def norm(i, _):
        parts = []
        for f in range(2):
            v = res[pl.ds(pl.multiple_of(128 * f + 16 * i, 16), 16), :].astype(F32)
            centred = v - jnp.mean(v, axis=-1, keepdims=True)
            variance = jnp.mean(centred * centred, axis=-1, keepdims=True)
            parts.append(centred * lax.rsqrt(variance + EPS) * (1.0 + mod_ref[2:3, :]) + mod_ref[1:2, :])
        for e in range(2):
            rows = slice(8 * e, 8 * e + 8)
            ns[2 * i + e, :, 0:D] = jnp.concatenate([parts[0][rows], parts[1][rows]], axis=0).astype(BF)
            ns[2 * i + e, :, D:TOK] = number
        return 0

    lax.fori_loop(0, 8, norm, 0)

    def to_owner(j):
        d = (chip + j) % CHIPS
        return copy(ns.at[d], xb.at[1, core, chip], a_s.at[j], a_r.at[chip], (z, d * 2 + core))

    def send_owner(j, _):
        to_owner(j).start()
        return 0

    lax.fori_loop(1, CHIPS, send_owner, 0)
    xb[1, core, chip] = ns[chip]

    def send_rest(i, _):
        for j in range(1, 4):
            across(2, (z + i) % NZ, j).start()
        return 0

    lax.fori_loop(1, 8, send_rest, 0)

    def batch(group, owner, g):
        return xb.at[group, owner, pl.ds(4 * g, 4)]

    def spread(g):
        here = batch(1, core, g)
        return (
            copy(here, batch(0, core, g), hs.at[0, g], hr.at[0, g], (up, seq)),
            copy(here, batch(2, core, g), hs.at[1, g], hr.at[1, g], (down, seq)),
            copy(here, here, ss.at[1, g], sr.at[1, g], (z, sib)),
        )

    def own_batch(g, _):
        for e in range(4):
            d = 4 * g + e

            @pl.when(d != chip)
            def _():
                copy(ns.at[d], xb.at[1, core, d], a_s.at[0], a_r.at[d], (z, sib)).wait_recv()

        for cp in spread(g):
            cp.start()
        return 0

    lax.fori_loop(0, 4, own_batch, 0)

    perm[...] = (frame_order(iota((512, 512), 1)) == iota((512, 512), 0)).astype(F32).astype(BF)
    perm_t[...] = (frame_order(iota((512, 512), 0)) == iota((512, 512), 1)).astype(F32).astype(BF)

    def wait_qkv(i, _):
        for j in range(1, 4):
            arrived(2, (z + i) % NZ, j)
        return 0

    lax.fori_loop(1, NZ, wait_qkv, 0)
    for q in range(4):
        for u in range(4):
            lanes = slice(128 * u, 128 * u + 128)
            wqkv[:, 512 * q + 128 * u : 512 * q + 128 * u + 128] = (
                wxq[q, :, :, lanes].astype(F32).reshape(D, 128).astype(BF)
            )

    def from_sib(group, g):
        there = batch(group, 1 - core, g)
        return copy(there, there, ss.at[group, g], sr.at[group, g], (z, sib))

    def sort_group(group):
        rows = xb[group].reshape(512, TOK)

        xp[group] = dot(perm[...], rows).astype(BF)

    def keys_values(group):
        def chunk(n, _):
            lanes = pl.ds(pl.multiple_of(256 * n, 128), 256)
            from_lanes = pl.ds(pl.multiple_of(HALF + 256 * n, 128), 256)
            made = dot(xp[group, :, 0:D], wqkv[:, from_lanes]).astype(BF)
            kv[:, 64 * group : 64 * group + 64, lanes] = made.reshape(POS, 64, 256)
            return 0

        lax.fori_loop(0, 5, chunk, 0)

    def wait_sib(group):
        for g in range(4):
            from_sib(group, g).wait_recv()

    wait_sib(1)
    sort_group(1)
    for low, wide in ((0, 256), (256, 256), (512, 128)):
        qs[:, low : low + wide] = dot(xp[1, :, 0:D], wqkv[:, low : low + wide]).astype(BF)
    keys_values(1)

    def relay(way, group, g):
        got = batch(group, core, g)
        return copy(got, got, ss.at[group, g], sr.at[group, g], (z, sib))

    for g in range(4):
        for way, group in ((0, 0), (1, 2)):
            got = batch(group, core, g)
            copy(got, got, hs.at[way, g], hr.at[way, g], (z, sib)).wait_recv()
            relay(way, group, g).start()
    for group in (0, 2):
        wait_sib(group)
        sort_group(group)
        keys_values(group)

    lane = iota((64, 128), 1)
    ids_q = xp[1, 0:64, D:TOK].astype(F32)
    ids_k = jnp.concatenate([xp[g, 0:64, D:TOK] for g in range(3)], axis=0).astype(F32)
    left = jnp.where(lane == 0, ids_q, jnp.where(lane == 1, 1.0, 0.0)).astype(BF)
    lane3 = iota((192, 128), 1)
    right = jnp.where(lane3 == 0, 1.0, jnp.where(lane3 == 1, -ids_k, 0.0)).astype(BF)
    apart = dot_t(left, right)
    same = jnp.concatenate([apart, apart], axis=0) == 0.0

    def position(p, _):
        rows = pl.ds(pl.multiple_of(64 * p, 64), 64)
        made = []
        for i in range(4):
            first, second = pair_masks(4 * core + i, 64)
            lanes = slice(128 * i, 128 * i + 256)
            q = qs[rows, lanes]
            k = kv[p, :, lanes]
            v = kv[p, :, HALF + 128 * i : HALF + 128 * i + 256]
            both = jnp.concatenate([q * first.astype(F32).astype(BF), q * second.astype(F32).astype(BF)], axis=0)
            scores = jnp.where(same, dot_t(both, k) * SCALE, NEG)
            o = dot(softmax(scores), v)
            made.append(jnp.where(first, o[:64], jnp.where(second, o[64:], 0.0)))
        tiles = [made[0][:, :128]]
        for i in range(1, 4):
            tiles.append(made[i - 1][:, 128:] + made[i][:, :128])
        tiles.append(made[3][:, 128:])
        for u in range(5):
            tt[rows, 128 * u : 128 * u + 128] = tiles[u].astype(BF)
        return 0

    lax.fori_loop(0, POS, position, 0)

    tb[...] = dot(perm_t[...], tt[...]).astype(BF).reshape(2, CHIPS, BLK, HALF)

    def to_frames(j):
        d = (seq + j) % 32
        return copy(tb.at[d % 2, d // 2], rb.at[core, chip], r_s.at[j], r_r.at[seq], (z, d))

    def send_back(j, _):
        to_frames(j).start()
        return 0

    lax.fori_loop(1, 32, send_back, 0)
    rb[core, chip] = tb[core, chip]

    def wait_back(j, _):
        d = (seq + j) % 32
        copy(tb.at[0, 0], rb.at[d % 2, d // 2], r_s.at[0], r_r.at[d], (z, sib)).wait_recv()
        return 0

    lax.fori_loop(1, 32, wait_back, 0)

    def finish(i, _):
        whole = []
        for e in range(2):
            a, b = rb[0, 2 * i + e].astype(F32), rb[1, 2 * i + e].astype(F32)
            whole.append(jnp.concatenate([a[:, :512], a[:, 512:] + b[:, :128], b[:, 128:]], axis=1))
        for f in range(2):
            rows = slice(8 * f, 8 * f + 8)
            temporal = jnp.concatenate([whole[0][rows], whole[1][rows]], axis=0)
            at = pl.multiple_of(16 * i, 16)
            kept = res[pl.ds(pl.multiple_of(128 * f + 16 * i, 16), 16), :].astype(F32)
            out_ref[f, pl.ds(at, 16), :] = (kept + mod_ref[3:4, :] * temporal).astype(BF)
        return 0

    lax.fori_loop(0, 8, finish, 0)

    for way, steps in ((0, 8), (1, 7)):
        for kind in range(3):

            def drain_ring(step, _):
                ring(kind, way, step, sent(way, step)).wait_send()
                return 0

            lax.fori_loop(0, steps, drain_ring, 0)

    def drain_across(i, _):
        for j in range(1, 4):
            across(0, (z + i) % NZ, j).wait_send()
            across(2, (z + i) % NZ, j).wait_send()
        return 0

    lax.fori_loop(1, NZ, drain_across, 0)
    to_sib.wait_send()

    def drain_owner(j, _):
        to_owner(j).wait_send()
        return 0

    lax.fori_loop(1, CHIPS, drain_owner, 0)

    def drain_batch(g, _):
        for cp in spread(g):
            cp.wait_send()
        relay(0, 0, g).wait_send()
        relay(1, 2, g).wait_send()
        return 0

    lax.fori_loop(0, 4, drain_batch, 0)

    def drain_back(j, _):
        to_frames(j).wait_send()
        return 0

    lax.fori_loop(1, 32, drain_back, 0)


def shards(hidden_states, spatial_qkv, spatial_out_weight, temporal_qkv_weight, modulation, video_ids):
    vmem = pl.BlockSpec(memory_space=pltpu.VMEM)
    dma = pltpu.SemaphoreType.DMA
    return pl.pallas_call(
        kernel,
        out_shape=jax.ShapeDtypeStruct(hidden_states.shape, BF),
        in_specs=[vmem] * 5 + [pl.BlockSpec(memory_space=pltpu.SMEM)],
        out_specs=vmem,
        scratch_shapes=[
            pltpu.VMEM((NZ, ROWS, 128), BF),
            pltpu.VMEM((2, 4, NZ, ROWS, 128), BF),
            pltpu.VMEM((4, NZ, ROWS, 512), BF),
            pltpu.VMEM((D, D), BF),
            pltpu.VMEM((D, 2048), BF),
            pltpu.VMEM((256, D), BF),
            pltpu.VMEM((256, D), BF),
            pltpu.VMEM((CHIPS, BLK, TOK), BF),
            pltpu.VMEM((3, 2, CHIPS, BLK, TOK), BF),
            pltpu.VMEM((3, 512, TOK), BF),
            pltpu.VMEM((512, HALF), BF),
            pltpu.VMEM((POS, 192, 2 * HALF), BF),
            pltpu.VMEM((512, HALF), BF),
            pltpu.VMEM((2, CHIPS, BLK, HALF), BF),
            pltpu.VMEM((2, CHIPS, BLK, HALF), BF),
            pltpu.VMEM((512, 512), BF),
            pltpu.VMEM((512, 512), BF),
            dma((2, 3, 8)),
            dma((2, 3, 8)),
            dma((NZ, 3)),
            dma((4, NZ)),
            dma((NZ, 3)),
            dma((4, NZ)),
            dma,
            dma,
            dma((CHIPS,)),
            dma((CHIPS,)),
            dma((2, 4)),
            dma((2, 4)),
            dma((3, 4)),
            dma((3, 4)),
            dma((32,)),
            dma((32,)),
        ],
        compiler_params=pltpu.CompilerParams(
            collective_id=0, has_side_effects=True, vmem_limit_bytes=58 * 2**20
        ),
        cost_estimate=pl.CostEstimate(flops=7_000_000_000, bytes_accessed=5_000_000, transcendentals=2_000_000),
    )(hidden_states, spatial_qkv, spatial_out_weight, temporal_qkv_weight, modulation, video_ids)


def solution(mesh):
    in_specs = (
        P(("dp", "seq"), None, None),
        P(("dp", "seq"), None, None),
        P("dp", None),
        P("dp", None),
        P(),
        P(("dp", "seq")),
    )
    out_specs = P(("dp", "seq"), None, None)
    return jax.shard_map(shards, mesh=mesh, in_specs=in_specs, out_specs=out_specs, check_vma=False)
```

```python
import math

import jax
import jax.numpy as jnp
from jax import lax
from jax.experimental import pallas as pl
from jax.experimental.pallas import tpu as pltpu
from jax.sharding import PartitionSpec as P

HEADS = 16
HD = 72
D = 1152
NEG = -1e30
EPS = 1e-06
SCALE = 1.0 / math.sqrt(HD)

NZ = 16
ROWS = 72
CHIPS = 16
POS = 8
BLK = 16
TOK = 1280
HALF = 640
PARTS = ((0, 256), (256, 384))
MESH = pl.DeviceIdType.MESH
BF = jnp.bfloat16
F32 = jnp.float32


def iota(shape, dim):
    return lax.broadcasted_iota(jnp.int32, shape, dim)


def dot(a, b):
    return jnp.dot(a, b, preferred_element_type=F32)


def dot_t(a, b):
    return lax.dot_general(a, b, (((1,), (1,)), ((), ())), preferred_element_type=F32)


def softmax(scores):
    top = jnp.max(scores, axis=-1, keepdims=True)
    powers = jnp.exp(scores - top)
    return (powers * (1.0 / jnp.sum(powers, axis=-1, keepdims=True))).astype(BF)


def pair_masks(pair, rows):
    lane = iota((rows, 256), 1)
    low = 16 * pair
    first = (lane >= low) & (lane < low + HD)
    second = (lane >= low + HD) & (lane < low + 2 * HD)
    return first, second


def sorted_place(rows):
    chip, two, pos = rows // 16, (rows % 16) // 8, rows % 8
    return pos * 8 + chip * 2 + two


def by_position(rows, p):
    return jnp.concatenate([rows[64 * b + 8 * p : 64 * b + 8 * p + 8] for b in range(rows.shape[0] // 64)], axis=0)


def kernel(
    hid_ref, qkv_ref, wo_ref, wt_ref, mod_ref, ids_ref, out_ref,
    w8, wxo, wxq, wout, wqkv, sp, res, ns, xa, xs, qs, kt, vs, tt, carry, tba, tbb, rba, rbb,
    zs, zr, xsq, xrq, zso, zro, xso, xro, zs8, zr8, xs8, xr8, ls, lr, a_s, a_r, hs, hr, ss, sr, r_s, r_r,
):
    z, seq = lax.axis_index("dp"), lax.axis_index("seq")
    core, chip = seq % 2, seq // 2
    x, y = chip // 4, chip % 4
    up, down, sib = (z + 1) % NZ, (z + NZ - 1) % NZ, chip * 2 + (1 - core)

    def copy(src, dst, send, recv, dev):
        return pltpu.make_async_remote_copy(
            src_ref=src, dst_ref=dst, send_sem=send, recv_sem=recv, device_id=dev, device_id_type=MESH
        )

    barrier = pltpu.get_barrier_semaphore()

    def greet(j, _):
        pl.semaphore_signal(barrier, inc=1, device_id=(z, (seq + j) % 32), device_id_type=MESH)
        return 0

    lax.fori_loop(1, 32, greet, 0)
    for dz in (1, 2, 4, 8, 12, 14, 15):
        pl.semaphore_signal(barrier, inc=1, device_id=((z + dz) % NZ, seq), device_id_type=MESH)

    for q in range(4):
        wxo[core, q, z] = wo_ref[:, pl.ds(pl.multiple_of(256 * q + 128 * core, 128), 128)]
        for u in range(4):
            n = min(4 * q + u, 14)
            lanes = pl.ds(pl.multiple_of((n // 5) * D + 128 * (n % 5) + 512 * core, 128), 128)
            wxq[q, z, :, 128 * u : 128 * u + 128] = wt_ref[:, lanes]

    @pl.when(z // 8 == core)
    def _():
        w8[z] = wo_ref[:, 1024:1152]

    sp[...] = jnp.zeros_like(sp)
    pl.semaphore_wait(barrier, 38)

    def quarter(k):
        odd = (k // 2) % 2
        return y * (1 - odd) + x * odd

    def has_last(k):
        return (quarter(k) == (k // 2) % 4) & (k // 8 == core)

    def ring(way, k):
        ref = wxq.at[quarter(k), k]
        return copy(ref, ref, zs, zr.at[k], (up, seq) if way == 0 else (down, seq))

    def sent(way, step):
        return (z + NZ - step) % NZ if way == 0 else (z + step) % NZ

    def neighbour(k, j):
        odd = (k // 2) % 2
        return (z, (((x + j * odd) % 4) * 4 + (y + j * (1 - odd)) % 4) * 2 + core)

    def across(k, j):
        ref = wxq.at[quarter(k), k]
        ahead = k % 2 if j == 1 else 1 - k % 2
        return copy(ref, ref, xsq, xrq.at[k * ahead + NZ * (1 - ahead)], neighbour(k, j))

    def hand_on(k):
        j = 3 - 2 * (k % 2)
        ref = wxq.at[(quarter(k) + 4 - j) % 4, k]
        copy(ref, ref, xsq, xrq.at[k], neighbour(k, j)).wait_recv()
        copy(ref, ref, xsq, xrq.at[NZ], neighbour(k, j)).start()

    def out_along(k, dz):
        ref = wxo.at[core, quarter(k), k]
        return copy(ref, ref, zso, zro.at[k], ((z + dz + NZ) % NZ, seq))

    def out_across(k, j):
        ref = wxo.at[core, quarter(k), k]
        return copy(ref, ref, xso, xro, neighbour(k, j))

    def last_along(k, dz):
        return copy(w8.at[k], w8.at[k], zs8, zr8.at[k], ((z + dz + NZ) % NZ, seq))

    def last_across(k, j):
        return copy(w8.at[k], w8.at[k], xs8, xr8.at[k], neighbour(k, j))

    def near(k):
        return (1, -1, 2 - 4 * ((k // 4) % 2))

    def send_near(k):
        for dz in near(k):
            out_along(k, dz).start()

        @pl.when(has_last(k))
        def _():
            for dz in near(k):
                last_along(k, dz).start()

    def send_across(k):
        for j in range(1, 4):
            out_across(k, j).start()

        @pl.when(has_last(k))
        def _():
            for j in range(1, 4):
                last_across(k, j).start()

    def wait_along(k):
        out_along(k, 1).wait_recv()

        @pl.when(has_last(k))
        def _():
            last_along(k, 1).wait_recv()

    def spatial_pair(f, pair):
        off = pl.multiple_of(128 * pair, 128)
        first, second = pair_masks(pair, 128)
        q = qkv_ref[f, :, pl.ds(off, 256)]
        k = qkv_ref[f, :, pl.ds(pl.multiple_of(D + off, 128), 256)]
        v = qkv_ref[f, :, pl.ds(pl.multiple_of(2 * D + off, 128), 256)]
        both = jnp.concatenate([q * first.astype(F32).astype(BF), q * second.astype(F32).astype(BF)], axis=0)
        o = dot(softmax(dot_t(both, k) * SCALE), v)
        rows = slice(128 * f, 128 * f + 128)
        old = sp[rows, pl.ds(off, 256)].astype(F32)
        sp[rows, pl.ds(off, 256)] = jnp.where(first, o[:128], jnp.where(second, o[128:], old)).astype(BF)

    def spatial_pairs(low, high):
        def one(i, _):
            for f in range(2):
                spatial_pair(f, i)
            return 0

        lax.fori_loop(low, high, one, 0)

    def ring_step(distance):
        for way in range(2 if distance < 8 else 1):
            k = sent(way, distance)
            ring(way, k).wait_recv()
            if distance not in (3, 7 + way, 8):
                ring(way, k).start()

    def ring_across(*distances):
        for j in (1, 3):
            for distance in distances:
                for way in range(2 if distance < 8 else 1):
                    across(sent(way, distance), j).start()

    def ring_hand_on(distance):
        for way in range(2 if distance < 8 else 1):
            hand_on(sent(way, distance))

    for dz in (8, 4, -4):
        out_along(z, dz).start()

    @pl.when(has_last(z))
    def _():
        for dz in (8, 4, -4):
            last_along(z, dz).start()

    send_near(z)
    for way in range(2):
        ring(way, z).start()

    for dz in (4, -4):
        ref = wxq.at[quarter(z), z]
        copy(ref, ref, zs, zr.at[z], ((z + dz + NZ) % NZ, seq)).start()
    spatial_pairs(0, 2)

    def far(i, _):
        k = (z + 4 + 8 * i - 12 * (i // 2)) % NZ
        wait_along(k)
        send_near(k)
        send_across(k)
        return 0

    lax.fori_loop(0, 3, far, 0)
    ring_step(1)
    ring_across(1)
    spatial_pairs(2, 6)

    def rest(i, _):
        k = (z + 4 * (i % 4) + 1 + i // 4) % NZ
        wait_along(k)
        send_across(k)
        return 0

    lax.fori_loop(0, 8, rest, 0)
    ring_step(4)
    ring_across(4)
    lax.fori_loop(8, 12, rest, 0)
    ring_step(2)
    ring_across(2)
    ring_hand_on(1)
    ring_step(5)
    ring_across(5)
    ring_step(3)
    ring_across(3)
    ring_hand_on(4)

    def wait_last(k, _):
        @pl.when((k != z) & (k // 8 == core) & (quarter(k) != (k // 2) % 4))
        def _():
            last_across(k, 1).wait_recv()

        return 0

    lax.fori_loop(0, NZ, wait_last, 0)
    pieces = wxo.at[core, pl.ds(0, 3), pl.ds(0, NZ - 1)]
    copy(pieces, pieces, xso, xro, (z, sib)).wait_recv()
    to_sib = copy(wxo.at[core], wxo.at[core], ls.at[0], lr.at[0], (z, sib))
    to_sib.start()
    mine, other = w8.at[pl.ds(8 * core, 8)], w8.at[pl.ds(8 * (1 - core), 8)]
    last_to_sib = copy(mine, mine, ls.at[1], lr.at[1], (z, sib))
    last_to_sib.start()
    spatial_pairs(6, 7)
    ring_step(6)
    ring_across(6)
    ring_hand_on(2)
    spatial_pairs(7, 8)
    copy(wxo.at[1 - core], wxo.at[1 - core], ls.at[0], lr.at[0], (z, sib)).wait_recv()
    copy(other, other, ls.at[1], lr.at[1], (z, sib)).wait_recv()

    for t in range(9):
        piece = w8[...] if t == 8 else wxo[t % 2, t // 2]
        wout[:, 128 * t : 128 * t + 128] = piece.astype(F32).reshape(D, 128).astype(BF)
    for low, wide in ((0, 256), (256, 256), (512, 256), (768, 256), (1024, 128)):
        lanes = slice(low, low + wide)
        projected = dot(sp[...], wout[:, lanes])
        res[:, lanes] = (
            hid_ref[:, :, lanes].reshape(256, wide).astype(F32) + mod_ref[0:1, lanes] * projected
        ).astype(BF)

    def to_owner(d):
        return copy(ns.at[d], xa.at[chip], a_s, a_r.at[chip // 4], (z, d * 2 + core))

    first_id, second_id = ids_ref[0].astype(F32), ids_ref[1].astype(F32)
    number = jnp.where(iota((BLK, 128), 0) < POS, first_id, second_id).astype(BF)

    def norm(step, _):
        i = (step + chip // 2) % 8
        parts = []
        for f in range(2):
            v = res[pl.ds(pl.multiple_of(128 * f + 16 * i, 16), 16), :].astype(F32)
            centred = v - jnp.mean(v, axis=-1, keepdims=True)
            variance = jnp.mean(centred * centred, axis=-1, keepdims=True)
            parts.append(centred * lax.rsqrt(variance + EPS) * (1.0 + mod_ref[2:3, :]) + mod_ref[1:2, :])
        for e in range(2):
            rows = slice(8 * e, 8 * e + 8)
            ns[2 * i + e, :, 0:D] = jnp.concatenate([parts[0][rows], parts[1][rows]], axis=0).astype(BF)
            ns[2 * i + e, :, D:TOK] = number

            @pl.when(2 * i + e != chip)
            def _():
                to_owner(2 * i + e).start()

        return 0

    lax.fori_loop(0, 8, norm, 0)

    xa[chip] = ns[chip]
    sort = (sorted_place(iota((64, 64), 1)) == iota((64, 64), 0)).astype(F32).astype(BF)
    unsort = (sorted_place(iota((64, 64), 0)) == iota((64, 64), 1)).astype(F32).astype(BF)
    ring_step(7)
    ring_across(7)
    ring_hand_on(5)

    def batch(group, owner, g):
        return xs.at[group, owner, g]

    def spread(g):
        here = batch(1, core, g)
        copy(here, batch(0, core, g), hs, hr.at[0, g], (up, seq)).start()
        copy(here, batch(2, core, g), hs, hr.at[1, g], (down, seq)).start()
        copy(here, here, ss, sr.at[1, g], (z, sib)).start()

    def own_batch(g):
        @pl.when(chip // 4 == g)
        def _():
            three = ns.at[pl.ds(0, 3)]
            copy(three, three, a_s, a_r.at[g], (z, sib)).wait_recv()

        @pl.when(chip // 4 != g)
        def _():
            four = ns.at[pl.ds(0, 4)]
            copy(four, four, a_s, a_r.at[g], (z, sib)).wait_recv()

        xs[1, core, g] = dot(sort, xa[pl.ds(4 * g, 4)].reshape(64, TOK)).astype(BF)
        spread(g)

    own_batch(0)
    ring_hand_on(3)
    own_batch(1)
    ring_step(8)
    ring_across(8)
    own_batch(2)
    ring_hand_on(6)
    own_batch(3)
    ring_hand_on(7)
    ring_hand_on(8)

    pieces = wxq.at[pl.ds(0, 2), pl.ds(0, NZ - 1)]
    copy(pieces, pieces, xsq, xrq.at[NZ], (z, sib)).wait_recv()
    for q in range(4):
        for u in range(4):
            lanes = slice(128 * u, 128 * u + 128)
            wqkv[:, 512 * q + 128 * u : 512 * q + 128 * u + 128] = (
                wxq[q, :, :, lanes].astype(F32).reshape(D, 128).astype(BF)
            )

    def wait_sib(group):
        for g in range(4):
            there = batch(group, 1 - core, g)
            copy(there, there, ss, sr.at[group, g], (z, sib)).wait_recv()

    def project(groups, low, wide):
        rows = [xs[group, :, :, :, 0:D].reshape(512, D) for group in groups]
        return dot(jnp.concatenate(rows, axis=0) if len(rows) > 1 else rows[0], wqkv[:, low : low + wide])

    def keys_values(groups, first_key):
        keys = slice(first_key, first_key + 64 * len(groups))
        for low, wide in ((0, 256), (256, 256), (512, 128)):
            made = project(groups, HALF + low, wide)
            for p in range(POS):
                kt[p, low : low + wide, keys] = by_position(made, p).T.astype(BF)
            made = project(groups, 2 * HALF + low, wide)
            for p in range(POS):
                vs[p, keys, low : low + wide] = by_position(made, p).astype(BF)

    wait_sib(1)
    for low, wide in ((0, 256), (256, 256), (512, 128)):
        made = project((1,), low, wide)
        for p in range(POS):
            qs[64 * p : 64 * p + 64, low : low + wide] = by_position(made, p).astype(BF)
    keys_values((1,), 128)

    def relay(group, g):
        got = batch(group, core, g)
        return copy(got, got, ss, sr.at[group, g], (z, sib))

    for g in range(4):
        for way, group in ((0, 0), (1, 2)):
            got = batch(group, core, g)
            copy(got, got, hs, hr.at[way, g], (z, sib)).wait_recv()
            relay(group, g).start()
    for group in (0, 2):
        wait_sib(group)
    keys_values((0, 2), 0)

    lane = iota((64, 128), 1)
    def ids_of(group):
        first = xs[group, :, :, 0:16, D:TOK].astype(F32)
        return jnp.concatenate([first[b // 4, b % 4, 0:8] for b in range(8)], axis=0)

    ids_q = ids_of(1)
    ids_k = jnp.concatenate([ids_of(0), ids_of(2), ids_q], axis=0)
    left = jnp.where(lane == 0, ids_q, jnp.where(lane == 1, 1.0, 0.0)).astype(BF)
    lane3 = iota((192, 128), 1)
    right = jnp.where(lane3 == 0, 1.0, jnp.where(lane3 == 1, -ids_k, 0.0)).astype(BF)
    apart = dot_t(left, right)
    same = jnp.concatenate([apart, apart], axis=0) == 0.0

    def send_back(part, made):
        low, wide = PARTS[part]
        for b in range(8):
            rows = dot(unsort, tt[b, :, low : low + wide].astype(BF)).astype(BF)
            made[4 * b : 4 * b + 4] = rows.reshape(4, BLK, wide)

        def one(j, _):
            d = (seq + j) % 32
            from_ref, to_ref = made.at[(d % 2) * CHIPS + d // 2], (rba, rbb)[part].at[core * CHIPS + chip]
            copy(from_ref, to_ref, r_s.at[part], r_r.at[part], (z, d)).start()
            return 0

        lax.fori_loop(1, 32, one, 0)
        (rba, rbb)[part][core * CHIPS + chip] = made[core * CHIPS + chip]

    for i in range(4):
        first, second = pair_masks(4 * core + i, 64)
        first_one, second_one = first.astype(F32).astype(BF), second.astype(F32).astype(BF)
        lanes = slice(128 * i, 128 * i + 256)

        def positions(step, _):
            for e in range(4):
                p = 4 * step + e
                rows = pl.ds(pl.multiple_of(64 * p, 64), 64)
                q = qs[rows, lanes]
                both = jnp.concatenate([q * first_one, q * second_one], axis=0)
                scores = jnp.where(same, dot(both, kt[p, lanes, :]) * SCALE, NEG)
                o = dot(softmax(scores), vs[p, :, lanes])
                made = jnp.where(first, o[:64], jnp.where(second, o[64:], 0.0))
                low = made[:, :128]
                if i > 0:
                    low = low + carry[rows, :]
                to = pl.ds(pl.multiple_of(8 * p, 8), 8)
                for b in range(8):
                    tt[b, to, 128 * i : 128 * i + 128] = low[8 * b : 8 * b + 8]
                    if i == 3:
                        tt[b, to, 512:640] = made[8 * b : 8 * b + 8, 128:]
                if i < 3:
                    carry[rows, :] = made[:, 128:]
            return 0

        lax.fori_loop(0, POS // 4, positions, 0)
        if i == 1:
            send_back(0, tba)

    send_back(1, tbb)
    for part, ref in ((0, rba), (1, rbb)):
        others = ref.at[pl.ds(0, 31)]
        copy(others, others, r_s.at[part], r_r.at[part], (z, sib)).wait_recv()

    def finish(i, _):
        whole = []
        for e in range(2):
            here, there = 2 * i + e, CHIPS + 2 * i + e
            low, low2 = rba[here].astype(F32), rba[there].astype(F32)
            high, high2 = rbb[here].astype(F32), rbb[there].astype(F32)
            whole.append(
                jnp.concatenate([low, high[:, :256], high[:, 256:] + low2[:, :128], low2[:, 128:], high2], axis=1)
            )
        for f in range(2):
            rows = slice(8 * f, 8 * f + 8)
            temporal = jnp.concatenate([whole[0][rows], whole[1][rows]], axis=0)
            at = pl.multiple_of(16 * i, 16)
            kept = res[pl.ds(pl.multiple_of(128 * f + 16 * i, 16), 16), :].astype(F32)
            out_ref[f, pl.ds(at, 16), :] = (kept + mod_ref[3:4, :] * temporal).astype(BF)
        return 0

    lax.fori_loop(0, 8, finish, 0)

    def drain(ref, sem):
        copy(ref, ref, sem, lr.at[0], (z, sib)).wait_send()

    drain(wxq.at[0, pl.ds(0, 15)], zs)
    drain(wxq.at[pl.ds(0, 3), pl.ds(0, 15)], xsq)
    drain(wxo.at[0, 0, pl.ds(0, 15)], zso)
    drain(wxo.at[0, pl.ds(0, 3), pl.ds(0, 15)], xso)

    def drain_last(k, _):
        @pl.when(has_last(k))
        def _():
            @pl.when((k - z + NZ) % 4 == 0)
            def _():
                drain(w8.at[pl.ds(0, 3)], zs8)

            @pl.when(k == z)
            def _():
                drain(w8.at[pl.ds(0, 3)], zs8)

            @pl.when(k != z)
            def _():
                drain(w8.at[pl.ds(0, 3)], xs8)

        return 0

    lax.fori_loop(0, NZ, drain_last, 0)
    to_sib.wait_send()
    last_to_sib.wait_send()
    drain(ns.at[pl.ds(0, 15)], a_s)
    drain(xs.at[0], hs)
    drain(xs.at[pl.ds(0, 3), 0], ss)
    drain(rba.at[pl.ds(0, 31)], r_s.at[0])
    drain(rbb.at[pl.ds(0, 31)], r_s.at[1])


def shards(hidden_states, spatial_qkv, spatial_out_weight, temporal_qkv_weight, modulation, video_ids):
    vmem = pl.BlockSpec(memory_space=pltpu.VMEM)
    dma = pltpu.SemaphoreType.DMA
    return pl.pallas_call(
        kernel,
        out_shape=jax.ShapeDtypeStruct(hidden_states.shape, BF),
        in_specs=[vmem] * 5 + [pl.BlockSpec(memory_space=pltpu.SMEM)],
        out_specs=vmem,
        scratch_shapes=[
            pltpu.VMEM((NZ, ROWS, 128), BF),
            pltpu.VMEM((2, 4, NZ, ROWS, 128), BF),
            pltpu.VMEM((4, NZ, ROWS, 512), BF),
            pltpu.VMEM((D, D), BF),
            pltpu.VMEM((D, 2048), BF),
            pltpu.VMEM((256, D), BF),
            pltpu.VMEM((256, D), BF),
            pltpu.VMEM((CHIPS, BLK, TOK), BF),
            pltpu.VMEM((CHIPS, BLK, TOK), BF),
            pltpu.VMEM((3, 2, 4, 64, TOK), BF),
            pltpu.VMEM((512, HALF), BF),
            pltpu.VMEM((POS, HALF, 192), BF),
            pltpu.VMEM((POS, 192, HALF), BF),
            pltpu.VMEM((8, 64, HALF), F32),
            pltpu.VMEM((512, 128), F32),
            pltpu.VMEM((32, BLK, 256), BF),
            pltpu.VMEM((32, BLK, 384), BF),
            pltpu.VMEM((32, BLK, 256), BF),
            pltpu.VMEM((32, BLK, 384), BF),
            dma,
            dma((NZ,)),
            dma,
            dma((NZ + 1,)),
            dma,
            dma((NZ,)),
            dma,
            dma,
            dma,
            dma((NZ,)),
            dma,
            dma((NZ,)),
            dma((2,)),
            dma((2,)),
            dma,
            dma((4,)),
            dma,
            dma((2, 4)),
            dma,
            dma((3, 4)),
            dma((2,)),
            dma((2,)),
        ],
        compiler_params=pltpu.CompilerParams(
            collective_id=0, has_side_effects=True, vmem_limit_bytes=58 * 2**20
        ),
        cost_estimate=pl.CostEstimate(flops=7_000_000_000, bytes_accessed=5_000_000, transcendentals=2_000_000),
    )(hidden_states, spatial_qkv, spatial_out_weight, temporal_qkv_weight, modulation, video_ids)


def solution(mesh):
    in_specs = (
        P(("dp", "seq"), None, None),
        P(("dp", "seq"), None, None),
        P("dp", None),
        P("dp", None),
        P(),
        P(("dp", "seq")),
    )
    out_specs = P(("dp", "seq"), None, None)
    return jax.shard_map(shards, mesh=mesh, in_specs=in_specs, out_specs=out_specs, check_vma=False)
```

```python
import math

import jax
import jax.numpy as jnp
from jax import lax
from jax.experimental import pallas as pl
from jax.experimental.pallas import tpu as pltpu
from jax.sharding import PartitionSpec as P

HEADS = 16
HD = 72
D = 1152
NEG = -1e30
EPS = 1e-06
SCALE = 1.0 / math.sqrt(HD)
LOG2E = math.log2(math.e)

NZ = 16
ROWS = 72
CHIPS = 16
POS = 8
BLK = 16
HALF = 640
PARTS = ((0, 256), (256, 384))
MESH = pl.DeviceIdType.MESH
BF = jnp.bfloat16
F32 = jnp.float32


def iota(shape, dim):
    return lax.broadcasted_iota(jnp.int32, shape, dim)


def dot(a, b):
    return jnp.dot(a, b, preferred_element_type=F32)


def dot_t(a, b):
    return lax.dot_general(a, b, (((1,), (1,)), ((), ())), preferred_element_type=F32)


def softmax(scores):
    top = jnp.max(scores, axis=-1, keepdims=True)
    powers = jnp.exp(scores - top)
    return (powers * (1.0 / jnp.sum(powers, axis=-1, keepdims=True))).astype(BF)


def pair_masks(pair, rows):
    lane = iota((rows, 256), 1)
    low = 16 * pair
    first = (lane >= low) & (lane < low + HD)
    second = (lane >= low + HD) & (lane < low + 2 * HD)
    return first, second


def sorted_place(rows):
    chip, two, pos = rows // 16, (rows % 16) // 8, rows % 8
    return pos * 8 + chip * 2 + two


def by_position(rows, p):
    return jnp.concatenate([rows[64 * b + 8 * p : 64 * b + 8 * p + 8] for b in range(rows.shape[0] // 64)], axis=0)


def kernel(
    hid_hbm, qkv_hbm, wo_ref, wt_ref, mod_ref, ids_ref, out_ref,
    hid_ref, qkv_ref, idb, idg, w8, wxo, wxq, wout, wqkv, sp, res, ns, xa, xs, qs, kt, vs, tt, carry, tba, tbb, rba, rbb,
    zs, zr, xsq, xrq, zso, zro, xso, xro, zs8, zr8, xs8, xr8, ls, lr, a_s, a_r, hs, hr, ss, sr, r_s, r_r, is_, ir, in_sem,
):
    get_qkv = pltpu.make_async_copy(qkv_hbm, qkv_ref, in_sem.at[0])
    get_hid = pltpu.make_async_copy(hid_hbm, hid_ref, in_sem.at[1])
    get_qkv.start()
    get_hid.start()
    z, seq = lax.axis_index("dp"), lax.axis_index("seq")
    core, chip = seq % 2, seq // 2
    x, y = chip // 4, chip % 4
    up, down, sib = (z + 1) % NZ, (z + NZ - 1) % NZ, chip * 2 + (1 - core)

    def copy(src, dst, send, recv, dev):
        return pltpu.make_async_remote_copy(
            src_ref=src, dst_ref=dst, send_sem=send, recv_sem=recv, device_id=dev, device_id_type=MESH
        )

    barrier = pltpu.get_barrier_semaphore()

    def greet(j, _):
        pl.semaphore_signal(barrier, inc=1, device_id=(z, (seq + j) % 32), device_id_type=MESH)
        return 0

    lax.fori_loop(1, 32, greet, 0)
    for dz in (1, 2, 4, 8, 12, 14, 15):
        pl.semaphore_signal(barrier, inc=1, device_id=((z + dz) % NZ, seq), device_id_type=MESH)

    for q in range(4):
        wxo[core, q, z] = wo_ref[:, pl.ds(pl.multiple_of(256 * q + 128 * core, 128), 128)]
        for u in range(4):
            n = min(4 * q + u, 14)
            lanes = pl.ds(pl.multiple_of((n // 5) * D + 128 * (n % 5) + 512 * core, 128), 128)
            wxq[q, z, :, 128 * u : 128 * u + 128] = wt_ref[:, lanes]

    @pl.when(z // 8 == core)
    def _():
        w8[z] = wo_ref[:, 1024:1152]

    sp[...] = jnp.zeros_like(sp)
    pl.semaphore_wait(barrier, 38)

    def quarter(k):
        odd = (k // 2) % 2
        return y * (1 - odd) + x * odd

    def has_last(k):
        return (quarter(k) == (k // 2) % 4) & (k // 8 == core)

    def ring(way, k):
        ref = wxq.at[quarter(k), k]
        return copy(ref, ref, zs, zr.at[k], (up, seq) if way == 0 else (down, seq))

    def sent(way, step):
        return (z + NZ - step) % NZ if way == 0 else (z + step) % NZ

    def neighbour(k, j):
        odd = (k // 2) % 2
        return (z, (((x + j * odd) % 4) * 4 + (y + j * (1 - odd)) % 4) * 2 + core)

    def across(k, j, direct=False):
        ref = wxq.at[quarter(k), k]
        ahead = 0 if direct else k % 2 if j == 1 else 1 - k % 2
        return copy(ref, ref, xsq, xrq.at[k * ahead + NZ * (1 - ahead)], neighbour(k, j))

    def hand_on(k):
        j = 3 - 2 * (k % 2)
        ref = wxq.at[(quarter(k) + 4 - j) % 4, k]
        copy(ref, ref, xsq, xrq.at[k], neighbour(k, j)).wait_recv()
        copy(ref, ref, xsq, xrq.at[NZ], neighbour(k, j)).start()

    def out_along(k, dz):
        ref = wxo.at[core, quarter(k), k]
        return copy(ref, ref, zso, zro.at[k], ((z + dz + NZ) % NZ, seq))

    def out_across(k, j):
        ref = wxo.at[core, quarter(k), k]
        return copy(ref, ref, xso, xro, neighbour(k, j))

    def last_along(k, dz):
        return copy(w8.at[k], w8.at[k], zs8, zr8.at[k], ((z + dz + NZ) % NZ, seq))

    def last_across(k, j):
        return copy(w8.at[k], w8.at[k], xs8, xr8.at[k], neighbour(k, j))

    def near(k):
        return (1, -1, 2 - 4 * ((k // 4) % 2))

    def send_near(k):
        for dz in near(k):
            out_along(k, dz).start()

        @pl.when(has_last(k))
        def _():
            for dz in near(k):
                last_along(k, dz).start()

    def send_across(k):
        for j in range(1, 4):
            out_across(k, j).start()

        @pl.when(has_last(k))
        def _():
            for j in range(1, 4):
                last_across(k, j).start()

    def wait_along(k):
        out_along(k, 1).wait_recv()

        @pl.when(has_last(k))
        def _():
            last_along(k, 1).wait_recv()

    def spatial_pair(f, pair):
        off = pl.multiple_of(128 * pair, 128)
        first, second = pair_masks(pair, 128)
        q = qkv_ref[f, :, pl.ds(off, 256)]
        k = qkv_ref[f, :, pl.ds(pl.multiple_of(D + off, 128), 256)]
        v = qkv_ref[f, :, pl.ds(pl.multiple_of(2 * D + off, 128), 256)]
        both = jnp.concatenate([q * first.astype(F32).astype(BF), q * second.astype(F32).astype(BF)], axis=0)
        o = dot(softmax(dot_t(both, k) * SCALE), v)
        rows = slice(128 * f, 128 * f + 128)
        old = sp[rows, pl.ds(off, 256)].astype(F32)
        sp[rows, pl.ds(off, 256)] = jnp.where(first, o[:128], jnp.where(second, o[128:], old)).astype(BF)

    def spatial_pairs(low, high):
        def one(i, _):
            for f in range(2):
                spatial_pair(f, i)
            return 0

        lax.fori_loop(low, high, one, 0)

    def ring_step(distance):
        for way in range(2 if distance < 8 else 1):
            k = sent(way, distance)
            ring(way, k).wait_recv()
            if distance not in (3, 7 + way, 8):
                ring(way, k).start()

    def ring_across(*distances):
        for j in (2, 1, 3):
            for distance in distances:
                for way in range(2 if distance < 8 else 1):
                    if j != 2 or distance >= 7:
                        across(sent(way, distance), j, distance >= 7).start()

    def ring_hand_on(distance):
        for way in range(2 if distance < 8 else 1):
            hand_on(sent(way, distance))

    for dz in (8, 4, -4):
        out_along(z, dz).start()

    @pl.when(has_last(z))
    def _():
        for dz in (8, 4, -4):
            last_along(z, dz).start()

    send_near(z)
    for way in range(2):
        ring(way, z).start()

    for dz in (4, -4):
        ref = wxq.at[quarter(z), z]
        copy(ref, ref, zs, zr.at[z], ((z + dz + NZ) % NZ, seq)).start()
    first_id, second_id = ids_ref[0].astype(F32), ids_ref[1].astype(F32)
    idb[core * CHIPS + chip] = jnp.where(iota((BLK, 128), 0) % 2 == 0, first_id, second_id).astype(BF)

    def send_ids(j, _):
        mine = idb.at[core * CHIPS + chip]
        copy(mine, mine, is_.at[0], ir.at[0], (z, (seq + j) % 32)).start()
        return 0

    lax.fori_loop(1, 32, send_ids, 0)
    get_qkv.wait()
    spatial_pairs(0, 2)

    def far(i, _):
        k = (z + 4 + 8 * i - 12 * (i // 2)) % NZ
        wait_along(k)
        send_near(k)
        send_across(k)
        return 0

    lax.fori_loop(0, 3, far, 0)
    ring_step(1)
    ring_across(1)
    spatial_pairs(2, 6)

    def rest(i, _):
        k = (z + 4 * (i % 4) + 1 + i // 4) % NZ
        wait_along(k)
        send_across(k)
        return 0

    lax.fori_loop(0, 8, rest, 0)
    ring_step(4)
    ring_across(4)
    lax.fori_loop(8, 12, rest, 0)
    ring_step(2)
    ring_across(2)
    ring_hand_on(1)
    others = idb.at[pl.ds(0, 31)]
    copy(others, others, is_.at[0], ir.at[0], (z, sib)).wait_recv()
    out_row, in_row = iota((64, 512), 0), iota((64, 512), 1)
    pick = (in_row == (out_row // 2) * BLK + out_row % 2).astype(F32).astype(BF)
    idg[1] = dot(pick, idb[...].reshape(512, 128)).astype(BF)
    copy(idg.at[1], idg.at[0], is_.at[1], ir.at[1], (up, seq)).start()
    copy(idg.at[1], idg.at[2], is_.at[1], ir.at[2], (down, seq)).start()
    ring_step(5)
    ring_across(5)
    ring_step(3)
    ring_across(3)
    ring_hand_on(4)

    def wait_last(k, _):
        @pl.when((k != z) & (k // 8 == core) & (quarter(k) != (k // 2) % 4))
        def _():
            last_across(k, 1).wait_recv()

        return 0

    lax.fori_loop(0, NZ, wait_last, 0)
    pieces = wxo.at[core, pl.ds(0, 3), pl.ds(0, NZ - 1)]
    copy(pieces, pieces, xso, xro, (z, sib)).wait_recv()
    to_sib = copy(wxo.at[core], wxo.at[core], ls.at[0], lr.at[0], (z, sib))
    to_sib.start()
    mine, other = w8.at[pl.ds(8 * core, 8)], w8.at[pl.ds(8 * (1 - core), 8)]
    last_to_sib = copy(mine, mine, ls.at[1], lr.at[1], (z, sib))
    last_to_sib.start()
    spatial_pairs(6, 7)
    ring_step(6)
    ring_across(6)
    ring_hand_on(2)
    spatial_pairs(7, 8)
    copy(wxo.at[1 - core], wxo.at[1 - core], ls.at[0], lr.at[0], (z, sib)).wait_recv()
    copy(other, other, ls.at[1], lr.at[1], (z, sib)).wait_recv()

    get_hid.wait()
    for t in range(9):
        piece = w8[...] if t == 8 else wxo[t % 2, t // 2]
        wout[:, 128 * t : 128 * t + 128] = piece.astype(F32).reshape(D, 128).astype(BF)
    for low, wide in ((0, 256), (256, 256), (512, 256), (768, 256), (1024, 128)):
        lanes = slice(low, low + wide)
        projected = dot(sp[...], wout[:, lanes])
        res[:, lanes] = (
            hid_ref[:, :, lanes].reshape(256, wide).astype(F32) + mod_ref[0:1, lanes] * projected
        ).astype(BF)

    def to_owner(d):
        return copy(ns.at[d], xa.at[chip], a_s, a_r.at[chip // 4], (z, d * 2 + core))

    def norm(step, _):
        i = (step + chip // 2) % 8
        parts = []
        for f in range(2):
            v = res[pl.ds(pl.multiple_of(128 * f + 16 * i, 16), 16), :].astype(F32)
            centred = v - jnp.mean(v, axis=-1, keepdims=True)
            variance = jnp.mean(centred * centred, axis=-1, keepdims=True)
            parts.append(centred * lax.rsqrt(variance + EPS) * (1.0 + mod_ref[2:3, :]) + mod_ref[1:2, :])
        for e in range(2):
            rows = slice(8 * e, 8 * e + 8)
            ns[2 * i + e] = jnp.concatenate([parts[0][rows], parts[1][rows]], axis=0).astype(BF)

            @pl.when(2 * i + e != chip)
            def _():
                to_owner(2 * i + e).start()

        return 0

    lax.fori_loop(0, 8, norm, 0)

    xa[chip] = ns[chip]
    sort = (sorted_place(iota((64, 64), 1)) == iota((64, 64), 0)).astype(F32).astype(BF)
    unsort = (sorted_place(iota((64, 64), 0)) == iota((64, 64), 1)).astype(F32).astype(BF)
    ring_step(7)
    ring_across(7)
    ring_hand_on(5)

    def batch(group, owner, g):
        return xs.at[group, owner, g]

    def spread(g):
        here = batch(1, core, g)
        copy(here, batch(0, core, g), hs, hr.at[0, g], (up, seq)).start()
        copy(here, batch(2, core, g), hs, hr.at[1, g], (down, seq)).start()
        copy(here, here, ss, sr.at[1, g], (z, sib)).start()

    def own_batch(g):
        @pl.when(chip // 4 == g)
        def _():
            three = ns.at[pl.ds(0, 3)]
            copy(three, three, a_s, a_r.at[g], (z, sib)).wait_recv()

        @pl.when(chip // 4 != g)
        def _():
            four = ns.at[pl.ds(0, 4)]
            copy(four, four, a_s, a_r.at[g], (z, sib)).wait_recv()

        xs[1, core, g] = dot(sort, xa[pl.ds(4 * g, 4)].reshape(64, D)).astype(BF)
        spread(g)

    own_batch(0)
    ring_hand_on(3)
    own_batch(1)
    ring_step(8)
    ring_across(8)
    own_batch(2)
    ring_hand_on(6)
    own_batch(3)

    pieces = wxq.at[pl.ds(0, 3), pl.ds(0, 11)]
    copy(pieces, pieces, xsq, xrq.at[NZ], (z, sib)).wait_recv()
    for q in range(4):
        for u in range(4):
            lanes = slice(128 * u, 128 * u + 128)
            wqkv[:, 512 * q + 128 * u : 512 * q + 128 * u + 128] = (
                wxq[q, :, :, lanes].astype(F32).reshape(D, 128).astype(BF)
            )

    def wait_sib(group):
        for g in range(4):
            there = batch(group, 1 - core, g)
            copy(there, there, ss, sr.at[group, g], (z, sib)).wait_recv()

    def project(rows, low, wide):
        return dot(rows, wqkv[:, low : low + wide])

    def keys_values(rows, first_key):
        keys = slice(first_key, first_key + rows.shape[0] // POS)
        for low, wide in ((0, 256), (256, 256), (512, 128)):
            made = project(rows, HALF + low, wide)
            for p in range(POS):
                kt[p, low : low + wide, keys] = by_position(made, p).T.astype(BF)
            made = project(rows, 2 * HALF + low, wide)
            for p in range(POS):
                vs[p, keys, low : low + wide] = by_position(made, p).astype(BF)

    wait_sib(1)
    for low, wide in ((0, 256), (256, 256), (512, 128)):
        made = project(xs[1].reshape(512, D), low, wide)
        for p in range(POS):
            qs[64 * p : 64 * p + 64, low : low + wide] = by_position(made, p).astype(BF)
    keys_values(xs[1].reshape(512, D), 128)

    def relay(group, g):
        got = batch(group, core, g)
        return copy(got, got, ss, sr.at[group, g], (z, sib))

    for g in range(4):
        for way, group in ((0, 0), (1, 2)):
            got = batch(group, core, g)
            copy(got, got, hs, hr.at[way, g], (z, sib)).wait_recv()
            relay(group, g).start()
    for group in (0, 2):
        wait_sib(group)
    keys_values(jnp.concatenate([xs[0].reshape(512, D), xs[2].reshape(512, D)], axis=0), 0)

    lane = iota((64, 128), 1)
    for way, group in ((0, 0), (1, 2)):
        copy(idg.at[group], idg.at[group], is_.at[1], ir.at[1 + way], (z, sib)).wait_recv()
    ids_q = idg[1].astype(F32)
    ids_k = jnp.concatenate([idg[0], idg[2], idg[1]], axis=0).astype(F32)
    left = jnp.where(lane == 0, ids_q, jnp.where(lane == 1, 1.0, 0.0)).astype(BF)
    lane3 = iota((192, 128), 1)
    right = jnp.where(lane3 == 0, 1.0, jnp.where(lane3 == 1, -ids_k, 0.0)).astype(BF)
    apart = dot_t(left, right)
    same = jnp.concatenate([apart, apart], axis=0) == 0.0

    def send_back(part, made):
        low, wide = PARTS[part]
        for b in range(8):
            rows = dot(unsort, tt[b, :, low : low + wide].astype(BF)).astype(BF)
            made[4 * b : 4 * b + 4] = rows.reshape(4, BLK, wide)

        def one(j, _):
            d = (seq + j) % 32
            from_ref, to_ref = made.at[(d % 2) * CHIPS + d // 2], (rba, rbb)[part].at[core * CHIPS + chip]
            copy(from_ref, to_ref, r_s.at[part], r_r.at[part], (z, d)).start()
            return 0

        lax.fori_loop(1, 32, one, 0)
        (rba, rbb)[part][core * CHIPS + chip] = made[core * CHIPS + chip]

    for i in range(4):
        first, second = pair_masks(4 * core + i, 64)
        first_one, second_one = first.astype(F32).astype(BF), second.astype(F32).astype(BF)
        lanes = slice(128 * i, 128 * i + 256)

        def positions(step, _):
            for e in range(4):
                p = 4 * step + e
                rows = pl.ds(pl.multiple_of(64 * p, 64), 64)
                q = qs[rows, lanes]
                both = jnp.concatenate([q * first_one, q * second_one], axis=0)
                scores = jnp.where(same, dot(both, kt[p, lanes, :]) * (SCALE * LOG2E), NEG)
                powers = jnp.exp2(scores - jnp.max(scores, axis=-1, keepdims=True))
                o = dot((powers * (1.0 / jnp.sum(powers, axis=-1, keepdims=True))).astype(BF), vs[p, :, lanes])
                made = jnp.where(first, o[:64], jnp.where(second, o[64:], 0.0))
                low = made[:, :128]
                if i > 0:
                    low = low + carry[rows, :]
                to = pl.ds(pl.multiple_of(8 * p, 8), 8)
                for b in range(8):
                    tt[b, to, 128 * i : 128 * i + 128] = low[8 * b : 8 * b + 8]
                    if i == 3:
                        tt[b, to, 512:640] = made[8 * b : 8 * b + 8, 128:]
                if i < 3:
                    carry[rows, :] = made[:, 128:]
            return 0

        lax.fori_loop(0, POS // 4, positions, 0)
        if i == 1:
            send_back(0, tba)

    send_back(1, tbb)
    for part, ref in ((0, rba), (1, rbb)):
        others = ref.at[pl.ds(0, 31)]
        copy(others, others, r_s.at[part], r_r.at[part], (z, sib)).wait_recv()

    def finish(i, _):
        whole = []
        for e in range(2):
            here, there = 2 * i + e, CHIPS + 2 * i + e
            low, low2 = rba[here].astype(F32), rba[there].astype(F32)
            high, high2 = rbb[here].astype(F32), rbb[there].astype(F32)
            whole.append(
                jnp.concatenate([low, high[:, :256], high[:, 256:] + low2[:, :128], low2[:, 128:], high2], axis=1)
            )
        for f in range(2):
            rows = slice(8 * f, 8 * f + 8)
            temporal = jnp.concatenate([whole[0][rows], whole[1][rows]], axis=0)
            at = pl.multiple_of(16 * i, 16)
            kept = res[pl.ds(pl.multiple_of(128 * f + 16 * i, 16), 16), :].astype(F32)
            out_ref[f, pl.ds(at, 16), :] = (kept + mod_ref[3:4, :] * temporal).astype(BF)
        return 0

    lax.fori_loop(0, 8, finish, 0)

    def drain(ref, sem):
        copy(ref, ref, sem, lr.at[0], (z, sib)).wait_send()

    drain(wxq.at[0, pl.ds(0, 15)], zs)
    drain(wxq.at[pl.ds(0, 3), pl.ds(0, 15)], xsq)
    drain(wxo.at[0, 0, pl.ds(0, 15)], zso)
    drain(wxo.at[0, pl.ds(0, 3), pl.ds(0, 15)], xso)

    def drain_last(k, _):
        @pl.when(has_last(k))
        def _():
            @pl.when((k - z + NZ) % 4 == 0)
            def _():
                drain(w8.at[pl.ds(0, 3)], zs8)

            @pl.when(k == z)
            def _():
                drain(w8.at[pl.ds(0, 3)], zs8)

            @pl.when(k != z)
            def _():
                drain(w8.at[pl.ds(0, 3)], xs8)

        return 0

    lax.fori_loop(0, NZ, drain_last, 0)
    to_sib.wait_send()
    last_to_sib.wait_send()
    drain(ns.at[pl.ds(0, 15)], a_s)
    drain(xs.at[0], hs)
    drain(xs.at[pl.ds(0, 3), 0], ss)
    drain(idb.at[pl.ds(0, 31)], is_.at[0])
    drain(idg.at[pl.ds(0, 2)], is_.at[1])
    drain(rba.at[pl.ds(0, 31)], r_s.at[0])
    drain(rbb.at[pl.ds(0, 31)], r_s.at[1])


def shards(hidden_states, spatial_qkv, spatial_out_weight, temporal_qkv_weight, modulation, video_ids):
    vmem = pl.BlockSpec(memory_space=pltpu.VMEM)
    dma = pltpu.SemaphoreType.DMA
    return pl.pallas_call(
        kernel,
        out_shape=jax.ShapeDtypeStruct(hidden_states.shape, BF),
        in_specs=[pl.BlockSpec(memory_space=pl.ANY)] * 2 + [vmem] * 3 + [pl.BlockSpec(memory_space=pltpu.SMEM)],
        out_specs=vmem,
        scratch_shapes=[
            pltpu.VMEM((2, 128, D), BF),
            pltpu.VMEM((2, 128, 3 * D), BF),
            pltpu.VMEM((32, BLK, 128), BF),
            pltpu.VMEM((3, 64, 128), BF),
            pltpu.VMEM((NZ, ROWS, 128), BF),
            pltpu.VMEM((2, 4, NZ, ROWS, 128), BF),
            pltpu.VMEM((4, NZ, ROWS, 512), BF),
            pltpu.VMEM((D, D), BF),
            pltpu.VMEM((D, 2048), BF),
            pltpu.VMEM((256, D), BF),
            pltpu.VMEM((256, D), BF),
            pltpu.VMEM((CHIPS, BLK, D), BF),
            pltpu.VMEM((CHIPS, BLK, D), BF),
            pltpu.VMEM((3, 2, 4, 64, D), BF),
            pltpu.VMEM((512, HALF), BF),
            pltpu.VMEM((POS, HALF, 192), BF),
            pltpu.VMEM((POS, 192, HALF), BF),
            pltpu.VMEM((8, 64, HALF), F32),
            pltpu.VMEM((512, 128), F32),
            pltpu.VMEM((32, BLK, 256), BF),
            pltpu.VMEM((32, BLK, 384), BF),
            pltpu.VMEM((32, BLK, 256), BF),
            pltpu.VMEM((32, BLK, 384), BF),
            dma,
            dma((NZ,)),
            dma,
            dma((NZ + 1,)),
            dma,
            dma((NZ,)),
            dma,
            dma,
            dma,
            dma((NZ,)),
            dma,
            dma((NZ,)),
            dma((2,)),
            dma((2,)),
            dma,
            dma((4,)),
            dma,
            dma((2, 4)),
            dma,
            dma((3, 4)),
            dma((2,)),
            dma((2,)),
            dma((2,)),
            dma((3,)),
            dma((2,)),
        ],
        compiler_params=pltpu.CompilerParams(
            collective_id=0, has_side_effects=True, vmem_limit_bytes=58 * 2**20
        ),
        cost_estimate=pl.CostEstimate(flops=7_000_000_000, bytes_accessed=5_000_000, transcendentals=2_000_000),
    )(hidden_states, spatial_qkv, spatial_out_weight, temporal_qkv_weight, modulation, video_ids)


def solution(mesh):
    in_specs = (
        P(("dp", "seq"), None, None),
        P(("dp", "seq"), None, None),
        P("dp", None),
        P("dp", None),
        P(),
        P(("dp", "seq")),
    )
    out_specs = P(("dp", "seq"), None, None)
    return jax.shard_map(shards, mesh=mesh, in_specs=in_specs, out_specs=out_specs, check_vma=False)
```

```python
import math

import jax
import jax.numpy as jnp
from jax import lax
from jax.experimental import pallas as pl
from jax.experimental.pallas import tpu as pltpu
from jax.sharding import PartitionSpec as P

HEADS = 16
HD = 72
D = 1152
NEG = -1e30
EPS = 1e-06
SCALE = 1.0 / math.sqrt(HD)
LOG2E = math.log2(math.e)

NZ = 16
ROWS = 72
CHIPS = 16
POS = 8
BLK = 16
HALF = 640
PARTS = ((0, 256), (256, 384))
MESH = pl.DeviceIdType.MESH
BF = jnp.bfloat16
F32 = jnp.float32


def iota(shape, dim):
    return lax.broadcasted_iota(jnp.int32, shape, dim)


def dot(a, b):
    return jnp.dot(a, b, preferred_element_type=F32)


def dot_t(a, b):
    return lax.dot_general(a, b, (((1,), (1,)), ((), ())), preferred_element_type=F32)


def softmax(scores):
    scores = scores * (SCALE * LOG2E)
    top = jnp.max(scores, axis=-1, keepdims=True)
    powers = jnp.exp2(scores - top)
    return (powers * (1.0 / jnp.sum(powers, axis=-1, keepdims=True))).astype(BF)


def pair_masks(pair, rows):
    lane = iota((rows, 256), 1)
    low = 16 * pair
    first = (lane >= low) & (lane < low + HD)
    second = (lane >= low + HD) & (lane < low + 2 * HD)
    return first, second


def sorted_place(rows):
    chip, two, pos = rows // 16, (rows % 16) // 8, rows % 8
    return pos * 8 + chip * 2 + two


def by_position(rows, p):
    return jnp.concatenate([rows[64 * b + 8 * p : 64 * b + 8 * p + 8] for b in range(rows.shape[0] // 64)], axis=0)


def kernel(
    hid_hbm, qkv_hbm, wo_ref, wt_ref, mod_ref, ids_ref, out_ref,
    hid_ref, qkv_ref, idb, idg, w8, wxo, wxq, wout, wqkv, sp, res, ns, xa, xs, qs, kt, vs, tt, carry, tba, tbb, rba, rbb,
    zs, zr, xsq, xrq, zso, zro, xso, xro, zs8, zr8, xs8, xr8, ls, lr, a_s, a_r, hs, hr, ss, sr, r_s, r_r, is_, ir, in_sem,
):
    get_qkv = pltpu.make_async_copy(qkv_hbm, qkv_ref, in_sem.at[0])
    get_hid = pltpu.make_async_copy(hid_hbm, hid_ref, in_sem.at[1])
    get_qkv.start()
    get_hid.start()
    z, seq = lax.axis_index("dp"), lax.axis_index("seq")
    core, chip = seq % 2, seq // 2
    x, y = chip // 4, chip % 4
    up, down, sib = (z + 1) % NZ, (z + NZ - 1) % NZ, chip * 2 + (1 - core)

    def copy(src, dst, send, recv, dev):
        return pltpu.make_async_remote_copy(
            src_ref=src, dst_ref=dst, send_sem=send, recv_sem=recv, device_id=dev, device_id_type=MESH
        )

    barrier = pltpu.get_barrier_semaphore()

    def greet(j, _):
        pl.semaphore_signal(barrier, inc=1, device_id=(z, (seq + j) % 32), device_id_type=MESH)
        return 0

    lax.fori_loop(1, 32, greet, 0)
    for dz in (1, 2, 4, 8, 12, 14, 15):
        pl.semaphore_signal(barrier, inc=1, device_id=((z + dz) % NZ, seq), device_id_type=MESH)

    for q in range(4):
        wxo[core, q, z] = wo_ref[:, pl.ds(pl.multiple_of(256 * q + 128 * core, 128), 128)]
        for u in range(4):
            n = min(4 * q + u, 14)
            lanes = pl.ds(pl.multiple_of((n // 5) * D + 128 * (n % 5) + 512 * core, 128), 128)
            wxq[q, z, :, 128 * u : 128 * u + 128] = wt_ref[:, lanes]

    @pl.when(z // 8 == core)
    def _():
        w8[z] = wo_ref[:, 1024:1152]

    sp[...] = jnp.zeros_like(sp)
    pl.semaphore_wait(barrier, 38)

    def quarter(k):
        odd = (k // 2) % 2
        return y * (1 - odd) + x * odd

    def has_last(k):
        return (quarter(k) == (k // 2) % 4) & (k // 8 == core)

    def ring(way, k):
        ref = wxq.at[quarter(k), k]
        return copy(ref, ref, zs, zr.at[k], (up, seq) if way == 0 else (down, seq))

    def sent(way, step):
        return (z + NZ - step) % NZ if way == 0 else (z + step) % NZ

    def neighbour(k, j):
        odd = (k // 2) % 2
        return (z, (((x + j * odd) % 4) * 4 + (y + j * (1 - odd)) % 4) * 2 + core)

    def across(k, j, direct=False):
        ref = wxq.at[quarter(k), k]
        ahead = 0 if direct else k % 2 if j == 1 else 1 - k % 2
        return copy(ref, ref, xsq, xrq.at[k * ahead + NZ * (1 - ahead)], neighbour(k, j))

    def hand_on(k):
        j = 3 - 2 * (k % 2)
        ref = wxq.at[(quarter(k) + 4 - j) % 4, k]
        copy(ref, ref, xsq, xrq.at[k], neighbour(k, j)).wait_recv()
        copy(ref, ref, xsq, xrq.at[NZ], neighbour(k, j)).start()

    def out_along(k, dz):
        ref = wxo.at[core, quarter(k), k]
        return copy(ref, ref, zso, zro.at[k], ((z + dz + NZ) % NZ, seq))

    def out_across(k, j):
        ref = wxo.at[core, quarter(k), k]
        return copy(ref, ref, xso, xro, neighbour(k, j))

    def last_along(k, dz):
        return copy(w8.at[k], w8.at[k], zs8, zr8.at[k], ((z + dz + NZ) % NZ, seq))

    def last_across(k, j):
        return copy(w8.at[k], w8.at[k], xs8, xr8.at[k], neighbour(k, j))

    def near(k):
        return (1, -1, 2 - 4 * ((k // 4) % 2))

    def send_near(k):
        for dz in near(k):
            out_along(k, dz).start()

        @pl.when(has_last(k))
        def _():
            for dz in near(k):
                last_along(k, dz).start()

    def send_across(k):
        for j in range(1, 4):
            out_across(k, j).start()

        @pl.when(has_last(k))
        def _():
            for j in range(1, 4):
                last_across(k, j).start()

    def wait_along(k):
        out_along(k, 1).wait_recv()

        @pl.when(has_last(k))
        def _():
            last_along(k, 1).wait_recv()

    def spatial_pair(f, pair):
        off = 128 * pair
        first, second = pair_masks(pair, 128)
        q = qkv_ref[f, :, pl.ds(off, 256)]
        k = qkv_ref[f, :, pl.ds(D + off, 256)]
        v = qkv_ref[f, :, pl.ds(2 * D + off, 256)]
        both = jnp.concatenate([q * first.astype(F32).astype(BF), q * second.astype(F32).astype(BF)], axis=0)
        o = dot(softmax(dot_t(both, k)), v)
        rows = slice(128 * f, 128 * f + 128)
        old = sp[rows, pl.ds(off, 256)].astype(F32)
        sp[rows, pl.ds(off, 256)] = jnp.where(first, o[:128], jnp.where(second, o[128:], old)).astype(BF)

    def spatial_pairs(low, high):
        for i in range(low, high):
            for f in range(2):
                spatial_pair(f, i)

    def ring_step(distance):
        for way in range(2 if distance < 8 else 1):
            k = sent(way, distance)
            ring(way, k).wait_recv()
            if distance not in (3, 7 + way, 8):
                ring(way, k).start()

    def ring_across(*distances):
        for j in (2, 1, 3):
            for distance in distances:
                for way in range(2 if distance < 8 else 1):
                    if j != 2 or distance >= 7:
                        across(sent(way, distance), j, distance >= 7).start()

    def ring_hand_on(distance):
        for way in range(2 if distance < 8 else 1):
            hand_on(sent(way, distance))

    for dz in (8, 4, -4):
        out_along(z, dz).start()

    @pl.when(has_last(z))
    def _():
        for dz in (8, 4, -4):
            last_along(z, dz).start()

    send_near(z)
    for way in range(2):
        ring(way, z).start()

    first_id, second_id = ids_ref[0].astype(F32), ids_ref[1].astype(F32)
    idb[core * CHIPS + chip] = jnp.where(iota((BLK, 128), 0) % 2 == 0, first_id, second_id).astype(BF)

    def send_ids(j, _):
        mine = idb.at[core * CHIPS + chip]
        copy(mine, mine, is_.at[0], ir.at[0], (z, (seq + j) % 32)).start()
        return 0

    lax.fori_loop(1, 32, send_ids, 0)
    get_qkv.wait()
    spatial_pairs(0, 2)

    def far(i, _):
        k = (z + 4 + 8 * i - 12 * (i // 2)) % NZ
        wait_along(k)
        send_near(k)
        send_across(k)
        return 0

    lax.fori_loop(0, 3, far, 0)
    for dz in (4, -4):
        ref = wxq.at[quarter(z), z]
        copy(ref, ref, zs, zr.at[z], ((z + dz + NZ) % NZ, seq)).start()
    ring_step(1)
    ring_across(1)
    spatial_pairs(2, 6)

    def rest(i, _):
        k = (z + 4 * (i % 4) + 1 + i // 4) % NZ
        wait_along(k)
        send_across(k)
        return 0

    lax.fori_loop(0, 12, rest, 0)
    ring_step(4)
    ring_across(4)
    ring_step(2)
    ring_across(2)
    ring_hand_on(1)
    others = idb.at[pl.ds(0, 31)]
    copy(others, others, is_.at[0], ir.at[0], (z, sib)).wait_recv()
    out_row, in_row = iota((64, 512), 0), iota((64, 512), 1)
    pick = (in_row == (out_row // 2) * BLK + out_row % 2).astype(F32).astype(BF)
    idg[1] = dot(pick, idb[...].reshape(512, 128)).astype(BF)
    copy(idg.at[1], idg.at[0], is_.at[1], ir.at[1], (up, seq)).start()
    copy(idg.at[1], idg.at[2], is_.at[1], ir.at[2], (down, seq)).start()
    ring_step(5)
    ring_across(5)

    def wait_last(k, _):
        @pl.when((k != z) & (k // 8 == core) & (quarter(k) != (k // 2) % 4))
        def _():
            last_across(k, 1).wait_recv()

        return 0

    lax.fori_loop(0, NZ, wait_last, 0)
    pieces = wxo.at[core, pl.ds(0, 3), pl.ds(0, NZ - 1)]
    copy(pieces, pieces, xso, xro, (z, sib)).wait_recv()
    to_sib = copy(wxo.at[core], wxo.at[core], ls.at[0], lr.at[0], (z, sib))
    to_sib.start()
    mine, other = w8.at[pl.ds(8 * core, 8)], w8.at[pl.ds(8 * (1 - core), 8)]
    last_to_sib = copy(mine, mine, ls.at[1], lr.at[1], (z, sib))
    last_to_sib.start()
    spatial_pairs(6, 7)
    ring_step(3)
    ring_across(3)
    ring_hand_on(4)
    spatial_pairs(7, 8)
    ring_step(6)
    ring_across(6)
    ring_hand_on(2)
    copy(wxo.at[1 - core], wxo.at[1 - core], ls.at[0], lr.at[0], (z, sib)).wait_recv()
    copy(other, other, ls.at[1], lr.at[1], (z, sib)).wait_recv()

    get_hid.wait()
    for t in range(9):
        piece = w8[...] if t == 8 else wxo[t % 2, t // 2]
        wout[:, 128 * t : 128 * t + 128] = piece.astype(F32).reshape(D, 128).astype(BF)
    for low, wide in ((0, 256), (256, 256), (512, 256), (768, 256), (1024, 128)):
        lanes = slice(low, low + wide)
        projected = dot(sp[...], wout[:, lanes])
        res[:, lanes] = (
            hid_ref[:, :, lanes].reshape(256, wide).astype(F32) + mod_ref[0:1, lanes] * projected
        ).astype(BF)

    def to_owner(d):
        return copy(ns.at[d], xa.at[chip], a_s, a_r.at[chip // 4], (z, d * 2 + core))

    def norm(step, _):
        i = (step + 2 * (chip // 4)) % 8
        parts = []
        for f in range(2):
            v = res[pl.ds(pl.multiple_of(128 * f + 16 * i, 16), 16), :].astype(F32)
            centred = v - jnp.mean(v, axis=-1, keepdims=True)
            variance = jnp.mean(centred * centred, axis=-1, keepdims=True)
            parts.append(centred * lax.rsqrt(variance + EPS) * (1.0 + mod_ref[2:3, :]) + mod_ref[1:2, :])
        for e in range(2):
            rows = slice(8 * e, 8 * e + 8)
            ns[2 * i + e] = jnp.concatenate([parts[0][rows], parts[1][rows]], axis=0).astype(BF)

            @pl.when(2 * i + e != chip)
            def _():
                to_owner(2 * i + e).start()

        return 0

    lax.fori_loop(0, 8, norm, 0)

    xa[chip] = ns[chip]
    sort = (sorted_place(iota((64, 64), 1)) == iota((64, 64), 0)).astype(F32).astype(BF)
    unsort = (sorted_place(iota((64, 64), 0)) == iota((64, 64), 1)).astype(F32).astype(BF)
    ring_step(7)
    ring_across(7)
    ring_hand_on(5)

    def batch(group, owner, g):
        return xs.at[group, owner, g]

    def spread(g):
        here = batch(1, core, g)
        copy(here, batch(0, core, g), hs, hr.at[0, g], (up, seq)).start()
        copy(here, batch(2, core, g), hs, hr.at[1, g], (down, seq)).start()
        copy(here, here, ss, sr.at[1, g], (z, sib)).start()

    def turn(i):
        return (chip // 4 + 4 - i) % 4

    def own_batch(i):
        g = turn(i)
        blocks = ns.at[pl.ds(0, 3 if i == 0 else 4)]
        copy(blocks, blocks, a_s, a_r.at[g], (z, sib)).wait_recv()
        xs[1, core, g] = dot(sort, xa[pl.ds(4 * g, 4)].reshape(64, D)).astype(BF)
        spread(g)

    own_batch(0)
    ring_hand_on(3)
    own_batch(1)
    ring_step(8)
    ring_across(8)
    own_batch(2)
    ring_hand_on(6)
    own_batch(3)

    pieces = wxq.at[pl.ds(0, 3), pl.ds(0, 11)]
    copy(pieces, pieces, xsq, xrq.at[NZ], (z, sib)).wait_recv()
    for q in range(4):
        for u in range(4):
            lanes = slice(128 * u, 128 * u + 128)
            wqkv[:, 512 * q + 128 * u : 512 * q + 128 * u + 128] = (
                wxq[q, :, :, lanes].astype(F32).reshape(D, 128).astype(BF)
            )

    def wait_sib(group):
        for g in range(4):
            there = batch(group, 1 - core, g)
            copy(there, there, ss, sr.at[group, g], (z, sib)).wait_recv()

    def project(rows, low, wide):
        return dot(rows, wqkv[:, low : low + wide])

    def keys_values(rows, first_key):
        keys = slice(first_key, first_key + rows.shape[0] // POS)
        for low, wide in ((0, 256), (256, 256), (512, 128)):
            made = project(rows, HALF + low, wide)
            for p in range(POS):
                kt[p, low : low + wide, keys] = by_position(made, p).T.astype(BF)
            made = project(rows, 2 * HALF + low, wide)
            for p in range(POS):
                vs[p, keys, low : low + wide] = by_position(made, p).astype(BF)

    wait_sib(1)
    for low, wide in ((0, 256), (256, 256), (512, 128)):
        made = project(xs[1].reshape(512, D), low, wide)
        for p in range(POS):
            qs[64 * p : 64 * p + 64, low : low + wide] = by_position(made, p).astype(BF)
    keys_values(xs[1].reshape(512, D), 128)

    def relay(group, g):
        got = batch(group, core, g)
        return copy(got, got, ss, sr.at[group, g], (z, sib))

    for i in range(4):
        g = turn(i)
        for way, group in ((0, 0), (1, 2)):
            got = batch(group, core, g)
            copy(got, got, hs, hr.at[way, g], (z, sib)).wait_recv()
            relay(group, g).start()
    for group in (0, 2):
        wait_sib(group)
    keys_values(jnp.concatenate([xs[0].reshape(512, D), xs[2].reshape(512, D)], axis=0), 0)

    lane = iota((64, 128), 1)
    for way, group in ((0, 0), (1, 2)):
        copy(idg.at[group], idg.at[group], is_.at[1], ir.at[1 + way], (z, sib)).wait_recv()
    ids_q = idg[1].astype(F32)
    ids_k = jnp.concatenate([idg[0], idg[2], idg[1]], axis=0).astype(F32)
    left = jnp.where(lane == 0, ids_q, jnp.where(lane == 1, 1.0, 0.0)).astype(BF)
    lane3 = iota((192, 128), 1)
    right = jnp.where(lane3 == 0, 1.0, jnp.where(lane3 == 1, -ids_k, 0.0)).astype(BF)
    apart = dot_t(left, right)
    same = jnp.concatenate([apart, apart], axis=0) == 0.0

    def send_back(part, made):
        low, wide = PARTS[part]
        for b in range(8):
            rows = dot(unsort, tt[b, :, low : low + wide].astype(BF)).astype(BF)
            made[4 * b : 4 * b + 4] = rows.reshape(4, BLK, wide)

        def one(j, _):
            d = (seq + j) % 32
            from_ref, to_ref = made.at[(d % 2) * CHIPS + d // 2], (rba, rbb)[part].at[core * CHIPS + chip]
            copy(from_ref, to_ref, r_s.at[part], r_r.at[part], (z, d)).start()
            return 0

        lax.fori_loop(1, 32, one, 0)
        (rba, rbb)[part][core * CHIPS + chip] = made[core * CHIPS + chip]

    for i in range(4):
        first, second = pair_masks(4 * core + i, 64)
        first_one, second_one = first.astype(F32).astype(BF), second.astype(F32).astype(BF)
        lanes = slice(128 * i, 128 * i + 256)

        def positions(step, _):
            for e in range(4):
                p = 4 * step + e
                rows = pl.ds(pl.multiple_of(64 * p, 64), 64)
                q = qs[rows, lanes]
                both = jnp.concatenate([q * first_one, q * second_one], axis=0)
                scores = jnp.where(same, dot(both, kt[p, lanes, :]) * (SCALE * LOG2E), NEG)
                powers = jnp.exp2(scores - jnp.max(scores, axis=-1, keepdims=True))
                o = dot((powers * (1.0 / jnp.sum(powers, axis=-1, keepdims=True))).astype(BF), vs[p, :, lanes])
                made = jnp.where(first, o[:64], jnp.where(second, o[64:], 0.0))
                low = made[:, :128]
                if i > 0:
                    low = low + carry[rows, :]
                to = pl.ds(pl.multiple_of(8 * p, 8), 8)
                for b in range(8):
                    tt[b, to, 128 * i : 128 * i + 128] = low[8 * b : 8 * b + 8]
                    if i == 3:
                        tt[b, to, 512:640] = made[8 * b : 8 * b + 8, 128:]
                if i < 3:
                    carry[rows, :] = made[:, 128:]
            return 0

        lax.fori_loop(0, POS // 4, positions, 0)
        if i == 1:
            send_back(0, tba)

    send_back(1, tbb)
    for part, ref in ((0, rba), (1, rbb)):
        others = ref.at[pl.ds(0, 31)]
        copy(others, others, r_s.at[part], r_r.at[part], (z, sib)).wait_recv()

    def finish(i, _):
        whole = []
        for e in range(2):
            here, there = 2 * i + e, CHIPS + 2 * i + e
            low, low2 = rba[here].astype(F32), rba[there].astype(F32)
            high, high2 = rbb[here].astype(F32), rbb[there].astype(F32)
            whole.append(
                jnp.concatenate([low, high[:, :256], high[:, 256:] + low2[:, :128], low2[:, 128:], high2], axis=1)
            )
        for f in range(2):
            rows = slice(8 * f, 8 * f + 8)
            temporal = jnp.concatenate([whole[0][rows], whole[1][rows]], axis=0)
            at = pl.multiple_of(16 * i, 16)
            kept = res[pl.ds(pl.multiple_of(128 * f + 16 * i, 16), 16), :].astype(F32)
            out_ref[f, pl.ds(at, 16), :] = (kept + mod_ref[3:4, :] * temporal).astype(BF)
        return 0

    lax.fori_loop(0, 8, finish, 0)

    def drain(ref, sem):
        copy(ref, ref, sem, lr.at[0], (z, sib)).wait_send()

    drain(wxq.at[0, pl.ds(0, 15)], zs)
    drain(wxq.at[pl.ds(0, 3), pl.ds(0, 15)], xsq)
    drain(wxo.at[0, 0, pl.ds(0, 15)], zso)
    drain(wxo.at[0, pl.ds(0, 3), pl.ds(0, 15)], xso)

    def drain_last(k, _):
        @pl.when(has_last(k))
        def _():
            @pl.when((k - z + NZ) % 4 == 0)
            def _():
                drain(w8.at[pl.ds(0, 3)], zs8)

            @pl.when(k == z)
            def _():
                drain(w8.at[pl.ds(0, 3)], zs8)

            @pl.when(k != z)
            def _():
                drain(w8.at[pl.ds(0, 3)], xs8)

        return 0

    lax.fori_loop(0, NZ, drain_last, 0)
    to_sib.wait_send()
    last_to_sib.wait_send()
    drain(ns.at[pl.ds(0, 15)], a_s)
    drain(xs.at[0], hs)
    drain(xs.at[pl.ds(0, 3), 0], ss)
    drain(idb.at[pl.ds(0, 31)], is_.at[0])
    drain(idg.at[pl.ds(0, 2)], is_.at[1])
    drain(rba.at[pl.ds(0, 31)], r_s.at[0])
    drain(rbb.at[pl.ds(0, 31)], r_s.at[1])


def shards(hidden_states, spatial_qkv, spatial_out_weight, temporal_qkv_weight, modulation, video_ids):
    vmem = pl.BlockSpec(memory_space=pltpu.VMEM)
    dma = pltpu.SemaphoreType.DMA
    return pl.pallas_call(
        kernel,
        out_shape=jax.ShapeDtypeStruct(hidden_states.shape, BF),
        in_specs=[pl.BlockSpec(memory_space=pl.ANY)] * 2 + [vmem] * 3 + [pl.BlockSpec(memory_space=pltpu.SMEM)],
        out_specs=vmem,
        scratch_shapes=[
            pltpu.VMEM((2, 128, D), BF),
            pltpu.VMEM((2, 128, 3 * D), BF),
            pltpu.VMEM((32, BLK, 128), BF),
            pltpu.VMEM((3, 64, 128), BF),
            pltpu.VMEM((NZ, ROWS, 128), BF),
            pltpu.VMEM((2, 4, NZ, ROWS, 128), BF),
            pltpu.VMEM((4, NZ, ROWS, 512), BF),
            pltpu.VMEM((D, D), BF),
            pltpu.VMEM((D, 2048), BF),
            pltpu.VMEM((256, D), BF),
            pltpu.VMEM((256, D), BF),
            pltpu.VMEM((CHIPS, BLK, D), BF),
            pltpu.VMEM((CHIPS, BLK, D), BF),
            pltpu.VMEM((3, 2, 4, 64, D), BF),
            pltpu.VMEM((512, HALF), BF),
            pltpu.VMEM((POS, HALF, 192), BF),
            pltpu.VMEM((POS, 192, HALF), BF),
            pltpu.VMEM((8, 64, HALF), F32),
            pltpu.VMEM((512, 128), F32),
            pltpu.VMEM((32, BLK, 256), BF),
            pltpu.VMEM((32, BLK, 384), BF),
            pltpu.VMEM((32, BLK, 256), BF),
            pltpu.VMEM((32, BLK, 384), BF),
            dma,
            dma((NZ,)),
            dma,
            dma((NZ + 1,)),
            dma,
            dma((NZ,)),
            dma,
            dma,
            dma,
            dma((NZ,)),
            dma,
            dma((NZ,)),
            dma((2,)),
            dma((2,)),
            dma,
            dma((4,)),
            dma,
            dma((2, 4)),
            dma,
            dma((3, 4)),
            dma((2,)),
            dma((2,)),
            dma((2,)),
            dma((3,)),
            dma((2,)),
        ],
        compiler_params=pltpu.CompilerParams(
            collective_id=0, has_side_effects=True, vmem_limit_bytes=58 * 2**20
        ),
        cost_estimate=pl.CostEstimate(flops=7_000_000_000, bytes_accessed=5_000_000, transcendentals=2_000_000),
    )(hidden_states, spatial_qkv, spatial_out_weight, temporal_qkv_weight, modulation, video_ids)


def solution(mesh):
    in_specs = (
        P(("dp", "seq"), None, None),
        P(("dp", "seq"), None, None),
        P("dp", None),
        P("dp", None),
        P(),
        P(("dp", "seq")),
    )
    out_specs = P(("dp", "seq"), None, None)
    return jax.shard_map(shards, mesh=mesh, in_specs=in_specs, out_specs=out_specs, check_vma=False)
```
